32 devices in a mesh: emb: 16 (over z, y, core), wide: 2 (over x).
Axes of the slice: x: 2, y: 2, z: 4, core: 2. Of those that a mesh axis runs over, the one named last changes fastest.
Arguments:
- tables: bfloat16 [512, 512, 256], P('emb'), may hold values from -3 to 3
- bag_ids: int32 [2, 64, 512, 4], P('wide', None, 'emb'), may hold values from 0 to 511
- bag_lengths: int32 [2, 64, 512], P('wide', None, 'emb'), may hold values from 1 to 4
- slot_field: int32 [512], replicated, may hold values from 0 to 511, each once
- proj_y: bfloat16 [512, 256], replicated, may hold values from -0.25 to 0.25
- proj_p: bfloat16 [128, 512], replicated, may hold values from -0.25 to 0.25
- linear_w: bfloat16 [384, 512], replicated, may hold values from -0.25 to 0.25
- fm_gain: float32 [256], replicated, may hold values from 0.5 to 1.5
- w_up: bfloat16 [8192, 256], P('wide'), may hold values from -0.375 to 0.375
- w_down: bfloat16 [8192, 256], P('wide'), may hold values from -0.0625 to 0.0625
- out_gain: float32 [256], replicated, may hold values from 0.5 to 1.5
- cotangent: bfloat16 [2, 64, 512, 256], P('wide', 'emb'), may hold values from -6 to 6
Outputs:
- layer_out: bfloat16 [2, 64, 512, 256], P('wide', 'emb')
- pooled_grad: bfloat16 [2, 64, 512, 256], P('wide', None, 'emb')
- grad_up: float32 [8192, 256], P('wide')
- grad_down: float32 [8192, 256], P('wide')
The draws below stay inside these ranges and needn't reach their ends.
Inputs may be any that keep to these rules, and one draw needn't show every extreme that they name: `bag_ids`: each id indexes a bucket of the table of its slot. `slot_field`: each field appears in exactly one slot.
All inputs are finite; a program needn't handle non-finite values.
Results may differ from the reference program's by a relative error of at most 0.008.
Values may be sent and summed in bfloat16 or wider, within the bound.
No kernel may reach another device: no remote copies, remote signals or barrier semaphores. Data moves between devices by JAX's collectives and lax.ppermute only.
A program may use at most 128 MiB of HBM per device.

```python
import math
import jax
import jax.numpy as jnp
import numpy as np
from jax import lax

E = 256
FIELDS = 512
K = 256
HID = 8192
NF = 128
B_DEV = 4
ROWS = 512
BAG = 4
NL = 384
GROUPS = 2
GROUP_B = 64


def set_ends(entries, rng, least, largest):
    index_at = [jax.random.randint(jax.random.fold_in(rng, axis), (), 0, length) for axis, length in enumerate(entries.shape)]
    widest = entries.shape.index(max(entries.shape))
    next_to = index_at[:widest] + [(index_at[widest] + 1) % entries.shape[widest]] + index_at[widest + 1:]
    return entries.at[tuple(index_at)].set(least).at[tuple(next_to)].set(largest)


def steps_of(key, extent, shards, smallest, top_value):
    level = 1.0
    for dim, blocks in shards:
        steps = jax.random.uniform(jax.random.fold_in(jax.random.fold_in(key, 6), dim), (blocks,), jnp.float32, smallest / len(shards), top_value / len(shards))
        level = level * jnp.repeat(jnp.exp(steps), extent[dim] // blocks).reshape((-1,) + (1,) * (len(extent) - 1 - dim))
    return level


def rank_bounds(count, lean):
    portions = [(1 << 20) // math.isqrt(rank ** lean) + 1 for rank in range(1, count + 1)]
    width = 1 + sum(portions) // (1 << 30)
    return np.cumsum(np.array([max(1, weight // width) for weight in portions]))


def skewed_ids(rng, shape, count, lean):
    grid = rank_bounds(count, lean)
    ticket = jax.random.randint(jax.random.fold_in(rng, 1), shape, 0, int(grid[count - 1]))
    rank = jnp.searchsorted(jnp.asarray(grid, jnp.int32), ticket, side="right")
    return jax.random.permutation(jax.random.fold_in(rng, 2), count)[rank].astype(jnp.int32)


def gaussian(key, dims, scale, bound, cuts=(), held_as=jnp.bfloat16):
    level = steps_of(key, dims, cuts, -0.22, 0.18) if cuts else 1.0
    values = jax.random.normal(key, dims, jnp.float32) * scale * level
    return jnp.minimum(jnp.maximum(values, -bound), bound).astype(held_as)


def setup_inputs(seed: int = 0) -> dict:
    streams_of = jax.random.split(jax.random.key(seed), 13)
    tables = gaussian(streams_of[0], (FIELDS, ROWS, E), 0.5, 3.0, ((0, 16),))
    bag_ids = set_ends(skewed_ids(streams_of[1], (GROUPS, GROUP_B, FIELDS, BAG), ROWS, 2), jax.random.fold_in(streams_of[1], 3), 0, ROWS - 1).astype(jnp.int32)
    bag_lengths = set_ends(jax.random.randint(streams_of[2], (GROUPS, GROUP_B, FIELDS), 1, BAG + 1), jax.random.fold_in(streams_of[2], 1), 1, BAG).astype(jnp.int32)
    slot_field = jax.random.permutation(streams_of[3], FIELDS).astype(jnp.int32)
    proj_y = gaussian(streams_of[4], (FIELDS, K), FIELDS ** -0.5, 0.25)
    proj_p = gaussian(streams_of[5], (NF, FIELDS), FIELDS ** -0.5, 0.25)
    linear_w = gaussian(streams_of[6], (NL, FIELDS), FIELDS ** -0.5, 0.25)
    fm_gain = jnp.clip(1.0 + 0.1 * jax.random.normal(streams_of[7], (K,), jnp.float32), 0.5, 1.5)
    w_up = gaussian(streams_of[8], (HID, K), K ** -0.5, 0.375, ((0, 2),))
    w_down = gaussian(streams_of[9], (HID, E), HID ** -0.5, 0.0625, ((0, 2),))
    out_gain = jnp.clip(1.0 + 0.1 * jax.random.normal(streams_of[10], (E,), jnp.float32), 0.5, 1.5)
    cotangent = gaussian(streams_of[11], (GROUPS, GROUP_B, FIELDS, E), 1.0, 6.0, ((0, 2), (1, 16)))
    return dict(tables=tables, bag_ids=bag_ids, bag_lengths=bag_lengths, slot_field=slot_field, proj_y=proj_y, proj_p=proj_p, linear_w=linear_w, fm_gain=fm_gain, w_up=w_up, w_down=w_down, out_gain=out_gain, cotangent=cotangent)


norm_eps = 1e-05

def mult(form, left, right):
    return jnp.einsum(form, left.astype(jnp.float32), right.astype(jnp.float32), precision=lax.Precision.HIGHEST)

def layer_norm(values):
    centre = lax.optimization_barrier(jnp.mean(values, axis=-1, keepdims=True))
    shifted = values - centre
    scale = lax.rsqrt(lax.optimization_barrier(jnp.mean(shifted * shifted, axis=-1, keepdims=True)) + norm_eps)
    return (shifted * scale, scale)

def norm_back(unit, scale, gain, upstream):
    scaled = upstream * gain
    return scale * (scaled - lax.optimization_barrier(jnp.mean(scaled, axis=-1, keepdims=True)) - unit * lax.optimization_barrier(jnp.mean(scaled * unit, axis=-1, keepdims=True)))

def silu_back(values):
    sigma = jax.nn.sigmoid(values)
    return sigma * (1.0 + values * (1.0 - sigma))

def pool_bags(tables, ids, lengths):
    field_index = jnp.arange(FIELDS, dtype=jnp.int32)[None, :, None]
    gathered = tables[field_index, ids]
    live = (jnp.arange(BAG, dtype=jnp.int32)[None, None, :] < lengths[:, :, None]).astype(jnp.float32)
    return lax.optimization_barrier(jnp.sum(gathered.astype(jnp.float32) * live[..., None], axis=2)).astype(jnp.bfloat16)

def reference(tables, bag_ids, bag_lengths, slot_field, proj_y, proj_p, linear_w, fm_gain, w_up, w_down, out_gain, cotangent):
    ids_blocks = bag_ids.reshape(-1, B_DEV, FIELDS, BAG)
    length_blocks = bag_lengths.reshape(-1, B_DEV, FIELDS)
    cot_blocks = cotangent.reshape(-1, B_DEV, FIELDS, E)

    def one_block(carry, inputs):
        up_total, down_total = carry
        ids_now, lengths_now, cot_now = inputs
        pooled = pool_bags(tables, ids_now, lengths_now)
        embeds = jnp.zeros_like(pooled).at[:, slot_field].set(pooled)
        crossed = mult('bfe,fk->bek', embeds, proj_y).astype(jnp.bfloat16)
        mixing = mult('nf,bfe->bne', proj_p, embeds).astype(jnp.bfloat16)
        inter = mult('bne,bek->bnk', mixing, crossed)
        inter_unit, inter_scale = layer_norm(inter)
        inter_norm = (inter_unit * fm_gain).astype(jnp.bfloat16)
        inter_rows = inter_norm.reshape(B_DEV * NF, K)
        gate_pre = mult('rk,hk->rh', inter_rows, w_up)
        hidden = jax.nn.silu(gate_pre).astype(jnp.bfloat16)
        ff_rows = mult('rh,he->re', hidden, w_down)
        linear_out = mult('lf,bfe->ble', linear_w, embeds)
        summed = jnp.concatenate([ff_rows.reshape(B_DEV, NF, E), linear_out], axis=1) + embeds.astype(jnp.float32)
        summed_unit, summed_scale = layer_norm(summed)
        layer_out = (summed_unit * out_gain).astype(jnp.bfloat16)
        grad_summed = norm_back(summed_unit, summed_scale, out_gain, cot_now.astype(jnp.float32))
        grad_ff = grad_summed[:, :NF].astype(jnp.bfloat16)
        grad_lin = grad_summed[:, NF:].astype(jnp.bfloat16)
        grad_ff_rows = grad_ff.reshape(B_DEV * NF, E)
        down_part = mult('rh,re->he', hidden, grad_ff_rows)
        grad_hidden = mult('re,he->rh', grad_ff_rows, w_down)
        grad_gate = (grad_hidden * silu_back(gate_pre)).astype(jnp.bfloat16)
        up_part = mult('rh,rk->hk', grad_gate, inter_rows)
        grad_norm = mult('rh,hk->rk', grad_gate, w_up).reshape(B_DEV, NF, K)
        grad_inter = norm_back(inter_unit, inter_scale, fm_gain, grad_norm).astype(jnp.bfloat16)
        grad_mixing = mult('bnk,bek->bne', grad_inter, crossed).astype(jnp.bfloat16)
        grad_crossed = mult('bne,bnk->bek', mixing, grad_inter).astype(jnp.bfloat16)
        grad_embeds = grad_summed + mult('lf,ble->bfe', linear_w, grad_lin) + mult('nf,bne->bfe', proj_p, grad_mixing) + mult('fk,bek->bfe', proj_y, grad_crossed)
        grad_embeds = grad_embeds.astype(jnp.bfloat16)
        slot_grads = grad_embeds[:, slot_field]
        return ((up_total + up_part, down_total + down_part), (layer_out, slot_grads))
    start_carry = (jnp.zeros((HID, K), jnp.float32), jnp.zeros((HID, E), jnp.float32))
    (grad_up, grad_down), (outs, grads) = lax.scan(one_block, start_carry, (ids_blocks, length_blocks, cot_blocks))
    layer_out = outs.reshape(GROUPS, GROUP_B, FIELDS, E)
    pooled_grad = grads.reshape(GROUPS, GROUP_B, FIELDS, E)
    return (layer_out, pooled_grad, grad_up, grad_down)
```

```python
import functools

import jax
import jax.numpy as jnp
from jax import lax
from jax.experimental import pallas as pl
from jax.experimental.pallas import tpu as pltpu
from jax.sharding import Mesh
from jax.sharding import PartitionSpec as P

norm_eps = 1e-05
VMEM_BYTES = 44 * 1024 * 1024
BF = jnp.bfloat16
F32 = jnp.float32
LANES = 128
EMB = ("z", "y", "core")


def params():
    return pltpu.CompilerParams(vmem_limit_bytes=VMEM_BYTES)


def nn(left, right):
    return lax.dot_general(left, right, (((1,), (0,)), ((), ())), preferred_element_type=F32)


def nt(left, right):
    return lax.dot_general(left, right, (((1,), (1,)), ((), ())), preferred_element_type=F32)


def tn(left, right):
    return lax.dot_general(left, right, (((0,), (0,)), ((), ())), preferred_element_type=F32)


def layer_norm(values):
    centre = jnp.mean(values, axis=-1, keepdims=True)
    shifted = values - centre
    scale = lax.rsqrt(jnp.mean(shifted * shifted, axis=-1, keepdims=True) + norm_eps)
    return (shifted * scale, scale)


def norm_back(unit, scale, gain, upstream):
    scaled = upstream * gain
    return scale * (
        scaled
        - jnp.mean(scaled, axis=-1, keepdims=True)
        - unit * jnp.mean(scaled * unit, axis=-1, keepdims=True)
    )


def pool_kernel(ids_ref, tables_ref, out_ref, sums):
    slots, samples, bag = ids_ref.shape
    buckets = tables_ref.shape[1]
    bucket = lax.broadcasted_iota(jnp.int32, (samples, buckets), 1)
    for s in range(slots):
        ids = ids_ref[s]
        count = jnp.zeros((samples, buckets), F32)
        for j in range(bag):
            count = count + jnp.where(ids[:, j : j + 1] == bucket, 1.0, 0.0)
        bags = nn(count.astype(BF), tables_ref[s])
        for c in range(sums.shape[0]):
            sums[c, pl.ds(s * samples, samples), :] = bags[:, c * LANES : (c + 1) * LANES]
    for c in range(sums.shape[0]):
        for b in range(samples):
            bag_sums = sums.at[c][pl.ds(b, slots, stride=samples), :]
            out_ref[b, :, c * LANES : (c + 1) * LANES] = bag_sums.astype(BF)


def pool_bags(tables, ids, lengths):
    slots, buckets, width = tables.shape
    samples, _, bag = ids.shape
    live = jnp.arange(bag, dtype=jnp.int32)[None, None, :] < lengths[:, :, None]
    masked = jnp.where(live, ids, -1).transpose(1, 0, 2)
    step = 16 if slots % 16 == 0 else slots
    return pl.pallas_call(
        pool_kernel,
        grid=(slots // step,),
        in_specs=[
            pl.BlockSpec((step, samples, bag), lambda g: (g, 0, 0)),
            pl.BlockSpec((step, buckets, width), lambda g: (g, 0, 0)),
        ],
        out_specs=pl.BlockSpec((samples, step, width), lambda g: (0, g, 0)),
        out_shape=jax.ShapeDtypeStruct((samples, slots, width), BF),
        scratch_shapes=[pltpu.VMEM((width // LANES, step * samples, LANES), F32)],
        compiler_params=params(),
        name="pool",
    )(masked, tables)


def front_kernel(rec, slot_row, proj_y, proj_p, gain, embeds, crossed, mixing, inter, rows):
    owners, samples, slots, width = rec.shape
    fields = owners * slots
    made = proj_p.shape[0]
    field = lax.broadcasted_iota(jnp.int32, (fields, fields), 0)
    place = jnp.where(field == slot_row[...], 1.0, 0.0).astype(BF)
    for b in range(samples):
        x = nn(place, rec[:, b].reshape(fields, width)).astype(BF)
        embeds[b] = x
        c = tn(x, proj_y[...]).astype(BF)
        crossed[b] = c
        m = nn(proj_p[...], x).astype(BF)
        mixing[b] = m
        v = nn(m, c)
        inter[pl.ds(b * made, made), :] = v
        unit, _ = layer_norm(v)
        rows[pl.ds(b * made, made), :] = (unit * gain[...]).astype(BF)


def linear_kernel(embeds, linear_w, linear_wt, gain, cot, layer_out, partial):
    samples = embeds.shape[0]
    made = linear_w.shape[0]
    first = embeds.shape[1] - made
    for b in range(samples):
        x = embeds[b]
        summed = nn(linear_w[...], x) + x[first:].astype(F32)
        unit, scale = layer_norm(summed)
        layer_out[b, :first] = jnp.zeros_like(layer_out[b, :first])
        layer_out[b, first:] = (unit * gain[...]).astype(BF)
        grad = norm_back(unit, scale, gain[...], cot[b, first:].astype(F32))
        back = nn(linear_wt[...], grad.astype(BF))
        partial[b, :first] = back[:first]
        partial[b, first:] = back[first:] + grad


def up_kernel(rows, w_up, w_down_t, hidden, slope, out, total):
    step = pl.program_id(0)
    tile = w_up.shape[0]
    part = 256
    gained = None
    for s in range(tile // part):
        at = pl.ds(s * part, part)
        gate = nt(w_up[at, :], rows[...])
        sig = 0.5 * jnp.tanh(0.5 * gate) + 0.5
        h = gate * sig
        hb = h.astype(BF)
        hidden[at, :] = hb
        slope[at, :] = (sig + h * (1.0 - sig)).astype(BF)
        term = nn(w_down_t[:, at], hb)
        gained = term if gained is None else gained + term

    @pl.when(step == 0)
    def _():
        total[...] = gained

    @pl.when(step > 0)
    def _():
        total[...] += gained

    @pl.when(step == pl.num_programs(0) - 1)
    def _():
        out[...] = total[...].T.astype(out.dtype)


def tile_of(units, count):
    return min(units, 1024 if count <= 1024 else 256)


def mlp_up(rows, w_up, w_down_t, kind, name):
    count, width = rows.shape
    units = w_up.shape[0]
    tile = tile_of(units, count)
    return pl.pallas_call(
        up_kernel,
        grid=(units // tile,),
        in_specs=[
            pl.BlockSpec((count, width), lambda g: (0, 0)),
            pl.BlockSpec((tile, width), lambda g: (g, 0)),
            pl.BlockSpec((width, tile), lambda g: (0, g)),
        ],
        out_specs=[
            pl.BlockSpec((tile, count), lambda g: (g, 0)),
            pl.BlockSpec((tile, count), lambda g: (g, 0)),
            pl.BlockSpec((count, width), lambda g: (0, 0)),
        ],
        out_shape=[
            jax.ShapeDtypeStruct((units, count), BF),
            jax.ShapeDtypeStruct((units, count), BF),
            jax.ShapeDtypeStruct((count, width), kind),
        ],
        scratch_shapes=[pltpu.VMEM((width, count), F32)],
        compiler_params=params(),
        name=name,
    )(rows, w_up, w_down_t)


def top_kernel(ff_own, ff_other, embeds, gain, cot, _, layer_out, grad, grad_ff):
    samples, made, width = embeds.shape
    for b in range(samples):
        at = pl.ds(b * made, made)
        summed = ff_own[at, :] + embeds[b].astype(F32)
        for w in range(ff_other.shape[0]):
            summed = summed + ff_other[w, at, :].astype(F32)
        unit, scale = layer_norm(summed)
        layer_out[b] = (unit * gain[...]).astype(BF)
        g = norm_back(unit, scale, gain[...], cot[b].astype(F32))
        grad[at, :] = g
        grad_ff[at, :] = g.astype(BF)


def back_kernel(grad_ff, w_down, w_up_t, slope, grad_gate, out, total):
    step = pl.program_id(0)
    tile = w_down.shape[0]
    part = 256
    gained = None
    for s in range(tile // part):
        at = pl.ds(s * part, part)
        g = (nt(w_down[at, :], grad_ff[...]) * slope[at, :].astype(F32)).astype(BF)
        grad_gate[at, :] = g
        term = nn(w_up_t[:, at], g)
        gained = term if gained is None else gained + term

    @pl.when(step == 0)
    def _():
        total[...] = gained

    @pl.when(step > 0)
    def _():
        total[...] += gained

    @pl.when(step == pl.num_programs(0) - 1)
    def _():
        out[...] = total[...].T.astype(out.dtype)


def mlp_back(grad_ff, w_down, w_up_t, slope, kind, name):
    count, width = grad_ff.shape
    units = w_down.shape[0]
    tile = tile_of(units, count)
    return pl.pallas_call(
        back_kernel,
        grid=(units // tile,),
        in_specs=[
            pl.BlockSpec((count, width), lambda g: (0, 0)),
            pl.BlockSpec((tile, width), lambda g: (g, 0)),
            pl.BlockSpec((width, tile), lambda g: (0, g)),
            pl.BlockSpec((tile, count), lambda g: (g, 0)),
        ],
        out_specs=[
            pl.BlockSpec((tile, count), lambda g: (g, 0)),
            pl.BlockSpec((count, width), lambda g: (0, 0)),
        ],
        out_shape=[
            jax.ShapeDtypeStruct((units, count), BF),
            jax.ShapeDtypeStruct((count, width), kind),
        ],
        scratch_shapes=[pltpu.VMEM((width, count), F32)],
        compiler_params=params(),
        name=name,
    )(grad_ff, w_down, w_up_t, slope)


def weight_kernel(left_own, left_other, right_own, right_other, out):
    out[...] = (
        nn(left_own[...], right_own[...]) + nn(left_other[...], right_other[...])
    ).astype(out.dtype)


def weight_grad(left_own, left_other, right_own, right_other, name):
    units, count = left_own.shape
    others = left_other.shape[1]
    width = right_own.shape[1]
    tile = tile_of(units, others)
    return pl.pallas_call(
        weight_kernel,
        grid=(units // tile,),
        in_specs=[
            pl.BlockSpec((tile, count), lambda g: (g, 0)),
            pl.BlockSpec((tile, others), lambda g: (g, 0)),
            pl.BlockSpec((count, width), lambda g: (0, 0)),
            pl.BlockSpec((others, width), lambda g: (0, 0)),
        ],
        out_specs=pl.BlockSpec((tile, width), lambda g: (g, 0)),
        out_shape=jax.ShapeDtypeStruct((units, width), BF),
        compiler_params=params(),
        name=name,
    )(left_own, left_other, right_own, right_other)


def tail_kernel(
    norm_own, norm_other, inter, gain, crossed, mixing, grad_top, partial, proj_y, proj_p_t, slot_col, out
):
    owners, samples, slots, width = out.shape
    fields = owners * slots
    made = mixing.shape[1]
    field = lax.broadcasted_iota(jnp.int32, (fields, fields), 1)
    place = jnp.where(field == slot_col[...], 1.0, 0.0).astype(BF)
    for b in range(samples):
        at = pl.ds(b * made, made)
        upstream = norm_own[at, :]
        for w in range(norm_other.shape[0]):
            upstream = upstream + norm_other[w, at, :].astype(F32)
        unit, scale = layer_norm(inter[at, :])
        grad_inter = norm_back(unit, scale, gain[...], upstream).astype(BF)
        grad_mixing = nt(grad_inter, crossed[b]).astype(BF)
        grad_crossed = tn(mixing[b], grad_inter).astype(BF)
        grad = partial[b] + nn(proj_p_t[...], grad_mixing) + nt(proj_y[...], grad_crossed)
        top = (grad[:made] + grad_top[at, :]).astype(BF)
        grad = jnp.concatenate([top, grad[made:].astype(BF)], axis=0)
        out[:, b] = nn(place, grad).astype(BF).reshape(owners, slots, width)


def whole(kernel, shapes, name, **options):
    return pl.pallas_call(
        kernel,
        out_shape=[jax.ShapeDtypeStruct(shape, kind) for shape, kind in shapes],
        compiler_params=params(),
        name=name,
        **options,
    )


def body(
    wide,
    tables,
    bag_ids,
    bag_lengths,
    slot_field,
    proj_y,
    proj_p,
    linear_w,
    fm_gain,
    w_up,
    w_down,
    out_gain,
    cotangent,
):
    fields, width = proj_y.shape[0], tables.shape[2]
    made = proj_p.shape[0]
    cot = cotangent[0]
    samples = cot.shape[0]
    count = samples * made
    gain_fm, gain_out = fm_gain[None, :], out_gain[None, :]
    shifts = range(1, wide)

    def send(value, shift):
        return lax.ppermute(value, "wide", [(i, (i + shift) % wide) for i in range(wide)])

    def spread(value):
        return jnp.concatenate([send(value, k) for k in shifts], axis=0)

    def give_back(value):
        blocks = value.reshape(wide - 1, count, width)
        return jnp.concatenate([send(blocks[k - 1 : k], wide - k) for k in shifts], axis=0)

    pooled = pool_bags(tables, bag_ids[0], bag_lengths[0])
    owners = pooled.shape[0] // samples
    slots = pooled.shape[1]
    received = lax.all_to_all(pooled, EMB, split_axis=0, concat_axis=0, tiled=True)
    received = received.reshape(owners, samples, slots, width)
    w_up_t, w_down_t = w_up.T, w_down.T
    linear_wt, proj_p_t = linear_w.T, proj_p.T

    embeds, crossed, mixing, inter, rows = whole(
        front_kernel,
        [
            ((samples, fields, width), BF),
            ((samples, width, proj_y.shape[1]), BF),
            ((samples, made, width), BF),
            ((count, width), F32),
            ((count, width), BF),
        ],
        "front",
    )(received, slot_field[None, :], proj_y, proj_p, gain_fm)
    rows_other = spread(rows)
    layer_out, partial = whole(
        linear_kernel,
        [((samples, fields, width), BF), ((samples, fields, width), F32)],
        "linear",
    )(embeds, linear_w, linear_wt, gain_out, cot)
    hidden, slope, ff = mlp_up(rows, w_up, w_down_t, F32, "up_own")
    hidden_other, slope_other, ff_away = mlp_up(rows_other, w_up, w_down_t, BF, "up_other")
    ff_other = give_back(ff_away)

    head = pl.BlockSpec((samples, made, width), lambda g: (0, 0, 0))
    full = pl.BlockSpec(memory_space=pltpu.VMEM)
    layer_out, grad_top, grad_ff = whole(
        top_kernel,
        [((samples, fields, width), BF), ((count, width), F32), ((count, width), BF)],
        "top",
        grid=(1,),
        in_specs=[full, full, head, full, head, pl.BlockSpec(memory_space=pl.ANY)],
        out_specs=[head, full, full],
        input_output_aliases={5: 0},
    )(ff, ff_other, embeds, gain_out, cot, layer_out)
    grad_ff_other = spread(grad_ff)
    grad_gate, norm_own = mlp_back(grad_ff, w_down, w_up_t, slope, F32, "back_own")
    grad_gate_other, norm_away = mlp_back(
        grad_ff_other, w_down, w_up_t, slope_other, BF, "back_other"
    )
    norm_other = give_back(norm_away)
    down_part = weight_grad(hidden, hidden_other, grad_ff, grad_ff_other, "grad_down")
    up_part = weight_grad(grad_gate, grad_gate_other, rows, rows_other, "grad_up")
    down = lax.psum(down_part, EMB).astype(F32)
    up = lax.psum(up_part, EMB).astype(F32)
    (slot_grads,) = whole(tail_kernel, [((owners, samples, slots, width), BF)], "tail")(
        norm_own,
        norm_other,
        inter,
        gain_fm,
        crossed,
        mixing,
        grad_top,
        partial,
        proj_y,
        proj_p_t,
        slot_field[:, None],
    )
    returned = lax.all_to_all(
        slot_grads.reshape(owners * samples, slots, width), EMB, split_axis=0, concat_axis=0, tiled=True
    )
    return (layer_out[None], returned[None], up, down)


def solution(mesh):
    emb, wide = mesh.shape["emb"], mesh.shape["wide"]
    near = 2 if emb % 2 == 0 else 1
    far = 4 if (emb // near) % 4 == 0 else 1
    split = Mesh(
        mesh.devices.reshape(far, emb // near // far, near, wide), ("z", "y", "core", "wide")
    )
    return jax.shard_map(
        functools.partial(body, wide),
        mesh=split,
        in_specs=(
            P(EMB, None, None),
            P("wide", None, EMB, None),
            P("wide", None, EMB),
            P(),
            P(),
            P(),
            P(),
            P(),
            P("wide", None),
            P("wide", None),
            P(),
            P("wide", EMB, None, None),
        ),
        out_specs=(
            P("wide", EMB, None, None),
            P("wide", None, EMB, None),
            P("wide", None),
            P("wide", None),
        ),
        check_vma=False,
    )
```

```python
import functools

import jax
import jax.numpy as jnp
from jax import lax
from jax.experimental import pallas as pl
from jax.experimental.pallas import tpu as pltpu
from jax.sharding import Mesh
from jax.sharding import PartitionSpec as P

norm_eps = 1e-05
VMEM_BYTES = 48 * 1024 * 1024
BF = jnp.bfloat16
F32 = jnp.float32
LANES = 128
EMB = ("z", "y", "core")


def params():
    return pltpu.CompilerParams(vmem_limit_bytes=VMEM_BYTES)


def nn(left, right):
    return lax.dot_general(left, right, (((1,), (0,)), ((), ())), preferred_element_type=F32)


def nt(left, right):
    return lax.dot_general(left, right, (((1,), (1,)), ((), ())), preferred_element_type=F32)


def tn(left, right):
    return lax.dot_general(left, right, (((0,), (0,)), ((), ())), preferred_element_type=F32)


def layer_norm(values):
    centre = jnp.mean(values, axis=-1, keepdims=True)
    shifted = values - centre
    scale = lax.rsqrt(jnp.mean(shifted * shifted, axis=-1, keepdims=True) + norm_eps)
    return (shifted * scale, scale)


def norm_back(unit, scale, gain, upstream):
    scaled = upstream * gain
    return scale * (
        scaled
        - jnp.mean(scaled, axis=-1, keepdims=True)
        - unit * jnp.mean(scaled * unit, axis=-1, keepdims=True)
    )


def pool_kernel(ids_ref, tables_ref, *refs):
    outs, sums = refs[:-1], refs[-1]
    slots, samples, bag = ids_ref.shape
    buckets = tables_ref.shape[1]
    here = outs[0].shape[1]
    bucket = lax.broadcasted_iota(jnp.int32, (samples, buckets), 1)
    for s in range(slots):
        ids = ids_ref[s]
        count = jnp.zeros((samples, buckets), F32)
        for j in range(bag):
            count = count + jnp.where(ids[:, j : j + 1] == bucket, 1.0, 0.0)
        bags = nn(count.astype(BF), tables_ref[s])
        for c in range(sums.shape[0]):
            sums[c, pl.ds(s * samples, samples), :] = bags[:, c * LANES : (c + 1) * LANES]
    for b in range(samples):
        owner, local = divmod(b, here * len(outs))
        out = outs[local // here]
        for c in range(sums.shape[0]):
            bag_sums = sums.at[c][pl.ds(b, slots, stride=samples), :]
            out[owner, local % here, :, c * LANES : (c + 1) * LANES] = bag_sums.astype(BF)


def pool_bags(tables, ids, lengths, owners, halves):
    slots, buckets, width = tables.shape
    samples, _, bag = ids.shape
    here = samples // owners // halves
    live = jnp.arange(bag, dtype=jnp.int32)[None, None, :] < lengths[:, :, None]
    masked = jnp.where(live, ids, -1).transpose(1, 0, 2)
    step = 16 if slots % 16 == 0 else slots
    return pl.pallas_call(
        pool_kernel,
        grid=(slots // step,),
        in_specs=[
            pl.BlockSpec((step, samples, bag), lambda g: (g, 0, 0)),
            pl.BlockSpec((step, buckets, width), lambda g: (g, 0, 0)),
        ],
        out_specs=[pl.BlockSpec((owners, here, step, width), lambda g: (0, 0, g, 0))] * halves,
        out_shape=[jax.ShapeDtypeStruct((owners, here, slots, width), BF)] * halves,
        scratch_shapes=[pltpu.VMEM((width // LANES, step * samples, LANES), F32)],
        compiler_params=params(),
        name="pool",
    )(masked, tables)


def const(*shape):
    return pl.BlockSpec(shape, lambda *_: (0,) * len(shape))


def by_sample(*shape):
    return pl.BlockSpec(shape, lambda b: (b,) + (0,) * (len(shape) - 1))


def front_kernel(rec, slot_row, proj_y, proj_p, gain, embeds, crossed, mixing, inter, rows, place):
    owners, _, slots, width = rec.shape
    fields = owners * slots

    @pl.when(pl.program_id(0) == 0)
    def _():
        field = lax.broadcasted_iota(jnp.int32, (fields, fields), 0)
        place[...] = jnp.where(field == slot_row[...], 1.0, 0.0).astype(BF)

    x = nn(place[...], rec[:, 0].reshape(fields, width)).astype(BF)
    embeds[0] = x
    c = tn(x, proj_y[...]).astype(BF)
    crossed[0] = c
    m = nn(proj_p[...], x).astype(BF)
    mixing[0] = m
    v = nn(m, c)
    inter[...] = v
    unit, _ = layer_norm(v)
    rows[...] = (unit * gain[...]).astype(BF)


def front(received, slot_field, proj_y, proj_p, gain, name):
    owners, here, slots, width = received.shape
    fields, rank = proj_y.shape
    made = proj_p.shape[0]
    return pl.pallas_call(
        front_kernel,
        grid=(here,),
        in_specs=[
            pl.BlockSpec((owners, 1, slots, width), lambda b: (0, b, 0, 0)),
            const(1, fields),
            const(fields, rank),
            const(made, fields),
            const(1, rank),
        ],
        out_specs=[
            by_sample(1, fields, width),
            by_sample(1, width, rank),
            by_sample(1, made, width),
            by_sample(made, rank),
            by_sample(made, rank),
        ],
        out_shape=[
            jax.ShapeDtypeStruct((here, fields, width), BF),
            jax.ShapeDtypeStruct((here, width, rank), BF),
            jax.ShapeDtypeStruct((here, made, width), BF),
            jax.ShapeDtypeStruct((here * made, rank), F32),
            jax.ShapeDtypeStruct((here * made, rank), BF),
        ],
        scratch_shapes=[pltpu.VMEM((fields, fields), BF)],
        compiler_params=params(),
        name=name,
    )(received, slot_field[None, :], proj_y, proj_p, gain)


def linear_kernel(embeds, linear_w, gain, cot, *refs):
    layer_out, partial = refs[-2:]
    made = linear_w.shape[0]
    first = embeds.shape[1] - made
    x = embeds[0]
    summed = nn(linear_w[...], x) + x[first:].astype(F32)
    unit, scale = layer_norm(summed)
    layer_out[0, :first] = jnp.zeros_like(layer_out[0, :first])
    layer_out[0, first:] = (unit * gain[...]).astype(BF)
    grad = norm_back(unit, scale, gain[...], cot[0, first:].astype(F32))
    back = tn(linear_w[...], grad.astype(BF))
    partial[0, :first] = back[:first]
    partial[0, first:] = back[first:] + grad


def linear(embeds, linear_w, gain, cot, layer_out, start, name):
    here, fields, width = embeds.shape
    at_sample = pl.BlockSpec((1, fields, width), lambda b: (start + b, 0, 0))
    filled = [] if layer_out is None else [layer_out]
    return pl.pallas_call(
        linear_kernel,
        grid=(here,),
        in_specs=[
            by_sample(1, fields, width),
            const(*linear_w.shape),
            const(1, width),
            at_sample,
        ]
        + [pl.BlockSpec(memory_space=pl.ANY)] * len(filled),
        out_specs=[at_sample, by_sample(1, fields, width)],
        out_shape=[
            jax.ShapeDtypeStruct(cot.shape, BF),
            jax.ShapeDtypeStruct((here, fields, width), F32),
        ],
        input_output_aliases={4: 0} if filled else {},
        compiler_params=params(),
        name=name,
    )(embeds, linear_w, gain, cot, *filled)


def activate(gate):
    sig = 0.5 * jnp.tanh(0.5 * gate) + 0.5
    h = gate * sig
    return (h.astype(BF), sig + h * (1.0 - sig))


def up_kernel(rows_own, rows_other, w_up, w_down, out_own, out_other, rows, total):
    step = pl.program_id(0)
    own = rows_own.shape[0]

    @pl.when(step == 0)
    def _():
        rows[:own] = rows_own[...]
        rows[own:] = rows_other[...]

    hidden, _ = activate(nt(w_up[...], rows[...]))
    term = tn(w_down[...], hidden)

    @pl.when(step == 0)
    def _():
        total[...] = term

    @pl.when(step > 0)
    def _():
        total[...] += term

    @pl.when(step == pl.num_programs(0) - 1)
    def _():
        out_own[...] = total[:, :own].T
        out_other[...] = total[:, own:].T.astype(BF)


def mlp_up(rows_own, rows_other, w_up, w_down, name):
    own, width = rows_own.shape
    other = rows_other.shape[0]
    units = w_up.shape[0]
    tile = min(units, 1024 if own + other <= 1024 else 256)
    return pl.pallas_call(
        up_kernel,
        grid=(units // tile,),
        in_specs=[
            const(own, width),
            const(other, width),
            pl.BlockSpec((tile, width), lambda g: (g, 0)),
            pl.BlockSpec((tile, width), lambda g: (g, 0)),
        ],
        out_specs=[const(own, width), const(other, width)],
        out_shape=[
            jax.ShapeDtypeStruct((own, width), F32),
            jax.ShapeDtypeStruct((other, width), BF),
        ],
        scratch_shapes=[
            pltpu.VMEM((own + other, width), BF),
            pltpu.VMEM((width, own + other), F32),
        ],
        compiler_params=params(),
        name=name,
    )(rows_own, rows_other, w_up, w_down)


def top_kernel(ff_own, ff_other, embeds, gain, cot, _, layer_out, grad, grad_ff):
    summed = ff_own[...] + embeds[0].astype(F32)
    for w in range(ff_other.shape[0]):
        summed = summed + ff_other[w].astype(F32)
    unit, scale = layer_norm(summed)
    layer_out[0] = (unit * gain[...]).astype(BF)
    g = norm_back(unit, scale, gain[...], cot[0].astype(F32))
    grad[...] = g
    grad_ff[...] = g.astype(BF)


def top(ff_own, ff_other, embeds, gain, cot, layer_out, start, made, name):
    here, _, width = embeds.shape
    count = here * made
    at_sample = pl.BlockSpec((1, made, width), lambda b: (start + b, 0, 0))
    return pl.pallas_call(
        top_kernel,
        grid=(here,),
        in_specs=[
            by_sample(made, width),
            pl.BlockSpec((ff_other.shape[0], made, width), lambda b: (0, b, 0)),
            by_sample(1, made, width),
            const(1, width),
            at_sample,
            pl.BlockSpec(memory_space=pl.ANY),
        ],
        out_specs=[at_sample, by_sample(made, width), by_sample(made, width)],
        out_shape=[
            jax.ShapeDtypeStruct(cot.shape, BF),
            jax.ShapeDtypeStruct((count, width), F32),
            jax.ShapeDtypeStruct((count, width), BF),
        ],
        input_output_aliases={5: 0},
        compiler_params=params(),
        name=name,
    )(ff_own, ff_other, embeds, gain, cot, layer_out)


def back_kernel(blocks, begun, last, _, *refs):
    rows_in, grads_in = refs[:blocks], refs[blocks : 2 * blocks]
    w_up, w_down = refs[2 * blocks : 2 * blocks + 2]
    refs = refs[2 * blocks + 2 :]
    if begun:
        before, refs = refs[0], refs[1:]
    grad_down, grad_up = refs[:2]
    outs = refs[2:-3] if last else refs[2:3]
    rows, grads = refs[-2:]
    total = refs[-3] if last else outs[0]
    step = pl.program_id(0)

    @pl.when(step == 0)
    def _():
        at = 0
        for row_block, grad_block in zip(rows_in, grads_in):
            count = row_block.shape[0]
            rows[at : at + count] = row_block[...]
            grads[at : at + count] = grad_block[...]
            at += count
        total[...] = before[...] if begun else jnp.zeros_like(total)

    shares, _, units, width = w_up.shape
    up = w_up[...].reshape(shares * units, width)
    down = w_down[...].reshape(shares * units, width)
    hidden, slope = activate(nt(up, rows[...]))
    gate = (nt(down, grads[...]) * slope).astype(BF)
    grad_down[...] = nn(hidden, grads[...]).astype(grad_down.dtype).reshape(shares, units, width)
    grad_up[...] = nn(gate, rows[...]).astype(grad_up.dtype).reshape(shares, units, width)
    total[...] += tn(up, gate)

    if last:

        @pl.when(step == pl.num_programs(0) - 1)
        def _():
            at = 0
            for out in outs:
                count = out.shape[0]
                out[...] = total[:, at : at + count].T.astype(out.dtype)
                at += count


def mlp_back(half, rows, grads, w_up, w_down, before, kind, row_kinds, name):
    shares, _, units, width = w_up.shape
    blocks = len(rows)
    count = sum(block.shape[0] for block in rows)
    last = row_kinds is not None
    step = max(1, min(shares, 512 // units if count <= 1024 else 128 // units))
    shared = pl.BlockSpec((step, 1, units, width), lambda g, at: (g, at[0], 0, 0))
    given = pl.BlockSpec((step, units, width), lambda g, at: (g, 0, 0))
    if last:
        outs = [jax.ShapeDtypeStruct(block.shape, k) for block, k in zip(rows, row_kinds)]
    else:
        outs = [jax.ShapeDtypeStruct((width, count), F32)]
    begun = [] if before is None else [before]
    return pl.pallas_call(
        functools.partial(back_kernel, blocks, bool(begun), last),
        grid_spec=pltpu.PrefetchScalarGridSpec(
            num_scalar_prefetch=1,
            grid=(shares // step,),
            in_specs=[const(*block.shape) for block in (*rows, *grads)]
            + [shared, shared]
            + [const(*block.shape) for block in begun],
            out_specs=[given, given] + [const(*out.shape) for out in outs],
            scratch_shapes=([pltpu.VMEM((width, count), F32)] if last else [])
            + [pltpu.VMEM((count, width), BF)] * 2,
        ),
        out_shape=[jax.ShapeDtypeStruct((shares, units, width), kind)] * 2 + outs,
        compiler_params=params(),
        name=name,
    )(half, *rows, *grads, w_up, w_down, *begun)


def split_kernel(count, each, at, *refs):
    ins, outs = refs[: -count * len(each)], refs[-count * len(each) :]
    for k in reversed(range(count)):
        here = lax.rem(at[0] + k, count)
        first = 0
        for n, terms in enumerate(each):
            total = ins[first][:, here].astype(F32)
            for ref in ins[first + 1 : first + terms]:
                total = total + ref[:, here].astype(F32)
            out = outs[n * count + k]
            out[...] = total.astype(out.dtype)
            first += terms


def split_sum(at, count, sums, kind, name):
    outs = []
    for arrays in sums:
        before, _, units, width = arrays[0].shape
        outs += [((before, units, width), kind if k == 0 else BF) for k in range(count)]
    pieces = whole(
        functools.partial(split_kernel, count, [len(arrays) for arrays in sums]),
        outs,
        name,
        in_specs=[pl.BlockSpec(memory_space=pltpu.SMEM)]
        + [pl.BlockSpec(memory_space=pltpu.VMEM)] * sum(len(arrays) for arrays in sums),
    )(at, *[array for arrays in sums for array in arrays])
    return [pieces[n * count : (n + 1) * count] for n in range(len(sums))]


def join_kernel(at, *refs):
    ins, out = refs[:-1], refs[-1]
    count = len(ins)
    for k, ref in enumerate(ins):
        out[:, lax.rem(at[0] + (count - k), count)] = ref[...].astype(out.dtype)


def join(at, arrays, kind, name):
    before, units, width = arrays[0].shape
    (out,) = whole(
        join_kernel,
        [((before, len(arrays), units, width), kind)],
        name,
        in_specs=[pl.BlockSpec(memory_space=pltpu.SMEM)]
        + [pl.BlockSpec(memory_space=pltpu.VMEM)] * len(arrays),
    )(at, *arrays)
    return out


def tail_kernel(
    norm_own, norm_other, inter, gain, crossed, mixing, grad_top, partial, proj_y, proj_p, slot_col, *refs
):
    out, place = refs[-2:]
    owners, _, slots, width = out.shape
    fields = owners * slots
    made = mixing.shape[1]

    @pl.when(pl.program_id(0) == 0)
    def _():
        field = lax.broadcasted_iota(jnp.int32, (fields, fields), 1)
        place[...] = jnp.where(field == slot_col[...], 1.0, 0.0).astype(BF)

    upstream = norm_own[...]
    for w in range(norm_other.shape[0]):
        upstream = upstream + norm_other[w].astype(F32)
    unit, scale = layer_norm(inter[...])
    grad_inter = norm_back(unit, scale, gain[...], upstream).astype(BF)
    grad_mixing = nt(grad_inter, crossed[0]).astype(BF)
    grad_crossed = tn(mixing[0], grad_inter).astype(BF)
    grad = partial[0] + tn(proj_p[...], grad_mixing) + nt(proj_y[...], grad_crossed)
    head = (grad[:made] + grad_top[...]).astype(BF)
    grad = jnp.concatenate([head, grad[made:].astype(BF)], axis=0)
    out[:, 0] = nn(place[...], grad).astype(BF).reshape(owners, slots, width)


def tail(own, other, kept, gain, proj_y, proj_p, slot_field, filled, start, shape, name):
    inter, crossed, mixing, grad_top, partial = kept
    owners, _, slots, width = shape
    here, fields, _ = partial.shape
    rank = proj_y.shape[1]
    made = mixing.shape[1]
    filled = [] if filled is None else [filled]
    return pl.pallas_call(
        tail_kernel,
        grid=(here,),
        in_specs=[
            by_sample(made, width),
            pl.BlockSpec((other.shape[0], made, width), lambda b: (0, b, 0)),
            by_sample(made, rank),
            const(1, rank),
            by_sample(1, width, rank),
            by_sample(1, made, width),
            by_sample(made, width),
            by_sample(1, fields, width),
            const(fields, rank),
            const(made, fields),
            const(fields, 1),
        ]
        + [pl.BlockSpec(memory_space=pl.ANY)] * len(filled),
        out_specs=pl.BlockSpec((owners, 1, slots, width), lambda b: (0, start + b, 0, 0)),
        out_shape=jax.ShapeDtypeStruct(shape, BF),
        scratch_shapes=[pltpu.VMEM((fields, fields), BF)],
        input_output_aliases={11: 0} if filled else {},
        compiler_params=params(),
        name=name,
    )(
        own,
        other,
        inter,
        gain,
        crossed,
        mixing,
        grad_top,
        partial,
        proj_y,
        proj_p,
        slot_field[:, None],
        *filled,
    )


def whole(kernel, shapes, name, **options):
    return pl.pallas_call(
        kernel,
        out_shape=[jax.ShapeDtypeStruct(shape, kind) for shape, kind in shapes],
        compiler_params=params(),
        name=name,
        **options,
    )


def turn(value, axis, size, shift):
    return lax.ppermute(value, axis, [(i, (i + shift) % size) for i in range(size)])


def after(value, *others):
    return lax.optimization_barrier((value, *others))[0]


def body(
    sizes,
    tables,
    bag_ids,
    bag_lengths,
    slot_field,
    proj_y,
    proj_p,
    linear_w,
    fm_gain,
    w_up,
    w_down,
    out_gain,
    cotangent,
):
    wide = sizes["wide"]
    near, mid, far = sizes["core"], sizes["y"], sizes["z"]
    owners = near * mid * far
    width = tables.shape[2]
    made = proj_p.shape[0]
    cot = cotangent[0]
    samples = cot.shape[0]
    halves = 2 if samples % 2 == 0 else 1
    here = samples // halves
    gain_fm, gain_out = fm_gain[None, :], out_gain[None, :]
    places = {axis: lax.axis_index(axis).astype(jnp.int32)[None] for axis in EMB}

    def spread(value):
        others = [turn(value, "wide", wide, k) for k in range(1, wide)]
        return others[0] if len(others) == 1 else jnp.concatenate(others, axis=0)

    def give_back(value):
        blocks = value.reshape(wide - 1, -1, width)
        others = [turn(blocks[k - 1 : k], "wide", wide, wide - k) for k in range(1, wide)]
        return others[0] if len(others) == 1 else jnp.concatenate(others, axis=0)

    def exchange(value):
        flat = value.reshape(owners * value.shape[1], *value.shape[2:])
        moved = lax.all_to_all(flat, EMB, split_axis=0, concat_axis=0, tiled=True)
        return moved.reshape(value.shape)

    pooled = pool_bags(tables, bag_ids[0], bag_lengths[0], owners, halves)
    received = [exchange(pooled[0])]
    for h in range(1, halves):
        received.append(exchange(after(pooled[h], received[h - 1])))
    kept, rows, rows_other, embeds, partial = [], [], [], [], []
    ff, ff_other, grad_top, grads, grads_other = [], [], [], [], []
    layer_out, made_last = None, None

    def forward(h):
        nonlocal layer_out, made_last
        mine = embeds[h]
        layer_out, part = linear(
            after(mine, made_last), linear_w, gain_out, cot, layer_out, h * here, f"linear_{h}"
        )
        partial.append(part)

    def finish(h):
        nonlocal layer_out, made_last
        layer_out, kept_grad, grad = top(
            ff[h], ff_other[h], embeds[h], gain_out, cot, layer_out, h * here, made, f"top_{h}"
        )
        grad_top.append(kept_grad)
        grads.append(grad)
        grads_other.append(spread(grad))
        made_last = grad

    for h in range(halves):
        got = received[h] if made_last is None else after(received[h], made_last)
        x, crossed, mixing, inter, row = front(got, slot_field, proj_y, proj_p, gain_fm, f"front_{h}")
        embeds.append(x)
        kept.append((inter, crossed, mixing))
        rows.append(row)
        rows_other.append(spread(row))
        made_last = row
        if h:
            forward(h - 1)
            finish(h - 1)
        own, away = mlp_up(
            rows[h] if not h else after(rows[h], made_last), rows_other[h], w_up, w_down, f"up_{h}"
        )
        ff.append(own)
        ff_other.append(give_back(away))
        made_last = away
    forward(halves - 1)
    finish(halves - 1)

    units = w_up.shape[0] // owners
    shared = (mid * far, near, units, width)
    up_shared, down_shared = w_up.reshape(shared), w_down.reshape(shared)
    count = len(rows)
    row_kinds = [F32] * count + [BF] * count
    total, parts_down, parts_up = None, [], []
    for k in reversed(range(near)):
        grad_down, grad_up, *outs = mlp_back(
            lax.rem(places["core"] + k, near),
            [*rows, *rows_other],
            [*grads, *grads_other],
            up_shared,
            down_shared,
            total,
            BF if k else F32,
            None if k else row_kinds,
            f"back_{k}",
        )
        total = outs[0]
        parts_down.insert(0, turn(grad_down, "core", near, k) if k else grad_down)
        parts_up.insert(0, turn(grad_up, "core", near, k) if k else grad_up)
    norm_own, norm_other = outs[:count], [give_back(away) for away in outs[count:]]

    cut = lambda arrays, size: [a.reshape(-1, size, units, width) for a in arrays]
    pieces = split_sum(places["y"], mid, [cut(parts_down, mid), cut(parts_up, mid)], F32, "split_y")
    sums = [[p[0]] + [turn(p[k], "y", mid, k) for k in range(1, mid)] for p in pieces]
    slot_grads, last = None, pieces[0][0]
    for h in range(halves):
        slot_grads = tail(
            after(norm_own[h], last),
            norm_other[h],
            (*kept[h], grad_top[h], partial[h]),
            gain_fm,
            proj_y,
            proj_p,
            slot_field,
            slot_grads,
            h * here,
            (owners, samples, *pooled[0].shape[2:]),
            f"tail_{h}",
        )
    returned = exchange(slot_grads)
    weights = []
    last = slot_grads
    for n, name in enumerate(("down", "up")):
        sums[n][0] = after(sums[n][0], last)
        (pieces,) = split_sum(places["z"], far, [cut(sums[n], far)], F32, f"{name}_split_z")
        last = pieces[0]
        sums[n] = [pieces[0]] + [turn(pieces[k], "z", far, k) for k in range(1, far)]
    for n, name in enumerate(("down", "up")):
        sums[n][0] = after(sums[n][0], last)
        (pieces,) = split_sum(places["z"], 1, [cut(sums[n], 1)], BF, f"{name}_share")
        last = pieces[0]
        weights.append(last)
    for axis, size in (("z", far), ("y", mid), ("core", near)):
        for n, name in enumerate(("down", "up")):
            parts = [weights[n]] + [turn(weights[n], axis, size, k) for k in range(1, size)]
            parts[0] = after(parts[0], last)
            kind = F32 if axis == "core" else BF
            last = join(places[axis], parts, kind, f"{name}_join_{axis}")
            weights[n] = last.reshape(-1, units, width)
    down, up = [w.reshape(-1, width) for w in weights]
    return (layer_out[None], returned.reshape(1, owners * samples, -1, width), up, down)


def solution(mesh):
    emb, wide = mesh.shape["emb"], mesh.shape["wide"]
    near = 2 if emb % 2 == 0 else 1
    far = 4 if (emb // near) % 4 == 0 else 1
    split = Mesh(
        mesh.devices.reshape(far, emb // near // far, near, wide), ("z", "y", "core", "wide")
    )
    return jax.shard_map(
        functools.partial(body, dict(split.shape)),
        mesh=split,
        in_specs=(
            P(EMB, None, None),
            P("wide", None, EMB, None),
            P("wide", None, EMB),
            P(),
            P(),
            P(),
            P(),
            P(),
            P("wide", None),
            P("wide", None),
            P(),
            P("wide", EMB, None, None),
        ),
        out_specs=(
            P("wide", EMB, None, None),
            P("wide", None, EMB, None),
            P("wide", None),
            P("wide", None),
        ),
        check_vma=False,
    )
```

```python
import functools

import jax
import jax.numpy as jnp
from jax import lax
from jax.experimental import pallas as pl
from jax.experimental.pallas import tpu as pltpu
from jax.sharding import Mesh
from jax.sharding import PartitionSpec as P

norm_eps = 1e-05
VMEM_BYTES = 24 * 1024 * 1024
BF = jnp.bfloat16
F32 = jnp.float32
LANES = 128
PART = 256


def params():
    return pltpu.CompilerParams(vmem_limit_bytes=VMEM_BYTES)


def ordered(kernel, ins, deps):
    return lambda *refs: kernel(*refs[:ins], *refs[ins + len(deps) :])


def unread(deps):
    return [pl.BlockSpec(memory_space=pl.ANY)] * len(deps)


def nn(left, right):
    return lax.dot_general(left, right, (((1,), (0,)), ((), ())), preferred_element_type=F32)


def nt(left, right):
    return lax.dot_general(left, right, (((1,), (1,)), ((), ())), preferred_element_type=F32)


def tn(left, right):
    return lax.dot_general(left, right, (((0,), (0,)), ((), ())), preferred_element_type=F32)


def layer_norm(values):
    centre = jnp.mean(values, axis=-1, keepdims=True)
    shifted = values - centre
    scale = lax.rsqrt(jnp.mean(shifted * shifted, axis=-1, keepdims=True) + norm_eps)
    return (shifted * scale, scale)


def norm_back(unit, scale, gain, upstream):
    scaled = upstream * gain
    return scale * (
        scaled
        - jnp.mean(scaled, axis=-1, keepdims=True)
        - unit * jnp.mean(scaled * unit, axis=-1, keepdims=True)
    )


def pool_kernel(ids_ref, tables_ref, *refs):
    outs, sums = refs[:-1], refs[-1]
    slots, samples, bag = ids_ref.shape
    buckets = tables_ref.shape[1]
    here = outs[0].shape[1]
    bucket = lax.broadcasted_iota(jnp.int32, (samples, buckets), 1)
    for s in range(slots):
        ids = ids_ref[s]
        count = jnp.zeros((samples, buckets), F32)
        for j in range(bag):
            count = count + jnp.where(ids[:, j : j + 1] == bucket, 1.0, 0.0)
        bags = nn(count.astype(BF), tables_ref[s])
        for c in range(sums.shape[0]):
            sums[c, pl.ds(s * samples, samples), :] = bags[:, c * LANES : (c + 1) * LANES]
    for b in range(samples):
        owner, local = divmod(b, here * len(outs))
        out = outs[local // here]
        for c in range(sums.shape[0]):
            bag_sums = sums.at[c][pl.ds(b, slots, stride=samples), :]
            out[owner, local % here, :, c * LANES : (c + 1) * LANES] = bag_sums.astype(BF)


def pool_bags(tables, ids, lengths, owners, halves):
    slots, buckets, width = tables.shape
    samples, _, bag = ids.shape
    here = samples // owners // halves
    live = jnp.arange(bag, dtype=jnp.int32)[None, None, :] < lengths[:, :, None]
    masked = jnp.where(live, ids, -1).transpose(1, 0, 2)
    step = 16 if slots % 16 == 0 else slots
    return pl.pallas_call(
        pool_kernel,
        grid=(slots // step,),
        in_specs=[
            pl.BlockSpec((step, samples, bag), lambda g: (g, 0, 0)),
            pl.BlockSpec((step, buckets, width), lambda g: (g, 0, 0)),
        ],
        out_specs=[pl.BlockSpec((owners, here, step, width), lambda g: (0, 0, g, 0))] * halves,
        out_shape=[jax.ShapeDtypeStruct((owners, here, slots, width), BF)] * halves,
        scratch_shapes=[pltpu.VMEM((width // LANES, step * samples, LANES), F32)],
        compiler_params=params(),
        name="pool",
    )(masked, tables)


def const(*shape):
    return pl.BlockSpec(shape, lambda *_: (0,) * len(shape))


def by_sample(*shape):
    return pl.BlockSpec(shape, lambda b: (b,) + (0,) * (len(shape) - 1))


def from_sample(start, *shape):
    return pl.BlockSpec(shape, lambda b: (start + b,) + (0,) * (len(shape) - 1))


def front_kernel(rec, slot_row, proj_y, proj_p, gain, *refs):
    embeds, crossed, mixing, inter, rows, place = refs[-6:]
    owners, _, slots, width = rec.shape
    fields = owners * slots

    @pl.when(pl.program_id(0) == 0)
    def _():
        field = lax.broadcasted_iota(jnp.int32, (fields, fields), 0)
        place[...] = jnp.where(field == slot_row[...], 1.0, 0.0).astype(BF)

    x = nn(place[...], rec[:, 0].reshape(fields, width)).astype(BF)
    embeds[0] = x
    c = tn(x, proj_y[...]).astype(BF)
    crossed[0] = c
    m = nn(proj_p[...], x).astype(BF)
    mixing[0] = m
    v = nn(m, c)
    inter[...] = v
    unit, _ = layer_norm(v)
    rows[...] = (unit * gain[...]).astype(BF)


def front(received, slot_field, proj_y, proj_p, gain, filled, samples, start, deps, name):
    owners, here, slots, width = received.shape
    fields, rank = proj_y.shape
    made = proj_p.shape[0]
    return pl.pallas_call(
        ordered(front_kernel, 5 + len(filled), deps),
        grid=(here,),
        in_specs=[
            pl.BlockSpec((owners, 1, slots, width), lambda b: (0, b, 0, 0)),
            const(1, fields),
            const(fields, rank),
            const(made, fields),
            const(1, rank),
        ]
        + unread(filled)
        + unread(deps),
        out_specs=[
            by_sample(1, fields, width),
            from_sample(start, 1, width, rank),
            from_sample(start, 1, made, width),
            from_sample(start, made, rank),
            by_sample(made, rank),
        ],
        out_shape=[
            jax.ShapeDtypeStruct((here, fields, width), BF),
            pltpu.HBM((samples, width, rank), BF),
            pltpu.HBM((samples, made, width), BF),
            pltpu.HBM((samples * made, rank), F32),
            jax.ShapeDtypeStruct((here * made, rank), BF),
        ],
        input_output_aliases={5: 1, 6: 2, 7: 3} if filled else {},
        scratch_shapes=[pltpu.VMEM((fields, fields), BF)],
        compiler_params=params(),
        name=name,
    )(received, slot_field[None, :], proj_y, proj_p, gain, *filled, *deps)


def linear_kernel(embeds, linear_w, gain, cot, before, layer_out, partial):
    made = linear_w.shape[0]
    first = embeds.shape[1] - made
    x = embeds[0]
    summed = nn(linear_w[...], x) + x[first:].astype(F32)
    unit, scale = layer_norm(summed)
    layer_out[0, :first] = before[0]
    layer_out[0, first:] = (unit * gain[...]).astype(BF)
    grad = norm_back(unit, scale, gain[...], cot[0, first:].astype(F32))
    back = tn(linear_w[...], grad.astype(BF))
    partial[0, :first] = back[:first]
    partial[0, first:] = back[first:] + grad


def linear(embeds, linear_w, gain, cot, top_out, deps):
    samples, fields, width = embeds.shape
    return pl.pallas_call(
        ordered(linear_kernel, 5, deps),
        grid=(samples,),
        in_specs=[
            by_sample(1, fields, width),
            const(*linear_w.shape),
            const(1, width),
            by_sample(1, fields, width),
            by_sample(1, top_out.shape[1], width),
        ]
        + unread(deps),
        out_specs=[by_sample(1, fields, width)] * 2,
        out_shape=[pltpu.HBM(cot.shape, BF), pltpu.HBM(cot.shape, F32)],
        compiler_params=params(),
        name="linear",
    )(embeds, linear_w, gain, cot, top_out, *deps)


def activate(gate):
    sig = 0.5 * jnp.tanh(0.5 * gate) + 0.5
    h = gate * sig
    return (h.astype(BF), sig + h * (1.0 - sig))


def tiles_of(weight, others, own, most):
    units, width = weight.shape
    tile = min(most, units)
    steps = units // tile
    specs = [
        pl.BlockSpec(
            (tile, width), lambda g, at, n=n: (jnp.clip(g - n * steps, 0, steps - 1), 0)
        )
        for n in range(own + len(others))
    ]
    return steps, specs


def tiles_at(steps, own, near, refs):
    step = pl.program_id(0)
    count = len(refs) // 2 - own
    up, down = (refs[0][...], refs[1][...]) if own else (None, None)
    for n in range(count):
        fetched, traded = refs[2 * own + n][...], refs[2 * own + count + n][...]
        far_up = jnp.where(near[0] == 0, fetched, traded)
        far_down = jnp.where(near[0] == 0, traded, fetched)
        here = step < (n + own) * steps
        up = far_up if up is None else jnp.where(here, up, far_up)
        down = far_down if down is None else jnp.where(here, down, far_down)
    return (up, down)


def accumulate(out, begun, term):
    @pl.when(pl.program_id(0) == 0)
    def _():
        out[...] = term if begun is None else begun[...] + term

    @pl.when(pl.program_id(0) > 0)
    def _():
        out[...] += term


def up_kernel(steps, own, begun, near, rows, *refs):
    up, down = tiles_at(steps, own, near, refs[begun:-1])
    term = None
    for at in range(0, up.shape[0], PART):
        hidden, _ = activate(nt(rows[...], up[at : at + PART]))
        more = nn(hidden, down[at : at + PART])
        term = more if term is None else term + more
    accumulate(refs[-1], refs[0] if begun else None, term)


def back_kernel(steps, own, begun, near, rows, grads, *refs):
    up, down = tiles_at(steps, own, near, refs[begun:-1])
    term = None
    for at in range(0, up.shape[0], PART):
        part = up[at : at + PART]
        _, slope = activate(nt(rows[...], part))
        more = nn((nt(grads[...], down[at : at + PART]) * slope).astype(BF), part)
        term = more if term is None else term + more
    accumulate(refs[-1], refs[0] if begun else None, term)


def mlp(kernel, near, blocks, w_up, w_down, fetched, traded, begun, deps, name, own=True):
    steps, specs = tiles_of(w_up, fetched, own, 1024)
    begun = [] if begun is None else [begun]
    weights = [w_up, w_down] if own else []
    ins = 1 + len(blocks) + len(begun) + len(weights) + 2 * len(fetched)
    return pl.pallas_call(
        ordered(functools.partial(kernel, steps, int(own), len(begun)), ins, deps),
        grid_spec=pltpu.PrefetchScalarGridSpec(
            num_scalar_prefetch=1,
            grid=(steps * len(specs),),
            in_specs=[const(*block.shape) for block in (*blocks, *begun)]
            + specs[:own] * 2
            + specs[own:] * 2
            + unread(deps),
            out_specs=const(*blocks[0].shape),
        ),
        out_shape=jax.ShapeDtypeStruct(blocks[0].shape, F32),
        compiler_params=params(),
        name=name,
    )(near, *blocks, *begun, *weights, *fetched, *traded, *deps)


def top_kernel(ff, embeds, gain, cot, layer_out, grad, grad_ff):
    summed = ff[...] + embeds[0].astype(F32)
    unit, scale = layer_norm(summed)
    layer_out[0] = (unit * gain[...]).astype(BF)
    g = norm_back(unit, scale, gain[...], cot[0].astype(F32))
    grad[...] = g
    grad_ff[...] = g.astype(BF)


def top(ff, embeds, gain, cot):
    samples, _, width = embeds.shape
    made = ff.shape[0] // samples
    return pl.pallas_call(
        top_kernel,
        grid=(samples,),
        in_specs=[
            by_sample(made, width),
            by_sample(1, made, width),
            const(1, width),
            by_sample(1, made, width),
        ],
        out_specs=[by_sample(1, made, width), by_sample(made, width), by_sample(made, width)],
        out_shape=[
            jax.ShapeDtypeStruct((samples, made, width), BF),
            jax.ShapeDtypeStruct(ff.shape, F32),
            jax.ShapeDtypeStruct(ff.shape, BF),
        ],
        compiler_params=params(),
        name="top",
    )(ff, embeds, gain, cot)


def fill(blocks, out):
    at = 0
    for block in blocks:
        out[at : at + block.shape[0]] = block[...]
        at += block.shape[0]


def weight_kernel(blocks, _, *refs):
    w_up, w_down, grad_down, grad_up, rows, grads = refs[2 * blocks :]

    @pl.when(pl.program_id(0) == 0)
    def _():
        fill(refs[:blocks], rows)
        fill(refs[blocks : 2 * blocks], grads)

    shares, units, width = grad_down.shape
    up = w_up[...].reshape(shares * units, width)
    down = w_down[...].reshape(shares * units, width)
    part = min(units * shares, PART)
    each = part // units
    for n in range(shares // each):
        at = slice(n * part, (n + 1) * part)
        hidden, slope = activate(nt(up[at], rows[...]))
        gate = (nt(down[at], grads[...]) * slope).astype(BF)
        for out, left, right in ((grad_down, hidden, grads), (grad_up, gate, rows)):
            grad = nn(left, right[...]).reshape(each, units, width)
            out[n * each : (n + 1) * each] = grad.astype(out.dtype)


def weight_grads(at, rows, grads, w_up, w_down, kind, deps, name):
    shares, _, units, width = w_up.shape
    blocks = len(rows)
    count = sum(block.shape[0] for block in rows)
    step = max(1, min(shares, 512 // units if count <= 1024 else 128 // units))
    shared = pl.BlockSpec((step, 1, units, width), lambda g, at: (g, at[0], 0, 0))
    given = pl.BlockSpec((step, units, width), lambda g, at: (g, 0, 0))
    return pl.pallas_call(
        ordered(functools.partial(weight_kernel, blocks), 1 + 2 * blocks + 2, deps),
        grid_spec=pltpu.PrefetchScalarGridSpec(
            num_scalar_prefetch=1,
            grid=(shares // step,),
            in_specs=[const(*block.shape) for block in (*rows, *grads)]
            + [shared, shared]
            + unread(deps),
            out_specs=[given, given],
            scratch_shapes=[pltpu.VMEM((count, width), BF)] * 2,
        ),
        out_shape=[jax.ShapeDtypeStruct((shares, units, width), kind)] * 2,
        compiler_params=params(),
        name=name,
    )(at, *rows, *grads, w_up, w_down, *deps)


def split_kernel(count, each, at, *refs):
    ins, outs = refs[: -count * len(each)], refs[-count * len(each) :]
    for k in reversed(range(count)):
        here = lax.rem(at[0] + k, count)
        first = 0
        for n, terms in enumerate(each):
            total = ins[first][:, here].astype(F32)
            for ref in ins[first + 1 : first + terms]:
                total = total + ref[:, here].astype(F32)
            out = outs[n * count + k]
            out[...] = total.astype(out.dtype)
            first += terms


def split_sum(at, count, sums, kind, deps, name):
    outs = []
    for arrays in sums:
        before, _, units, width = arrays[0].shape
        outs += [((before, units, width), kind if k == 0 else BF) for k in range(count)]
    each = [len(arrays) for arrays in sums]
    pieces = whole(
        ordered(functools.partial(split_kernel, count, each), 1 + sum(each), deps),
        outs,
        name,
        in_specs=[pl.BlockSpec(memory_space=pltpu.SMEM)]
        + [pl.BlockSpec(memory_space=pltpu.VMEM)] * sum(each)
        + unread(deps),
    )(at, *[array for arrays in sums for array in arrays], *deps)
    return [pieces[n * count : (n + 1) * count] for n in range(len(sums))]


def join_kernel(at, *refs):
    ins, out = refs[:-1], refs[-1]
    count = len(ins)
    for k, ref in enumerate(ins):
        out[:, lax.rem(at[0] + (count - k), count)] = ref[...].astype(out.dtype)


def join(at, arrays, kind, deps, name):
    before, units, width = arrays[0].shape
    (out,) = whole(
        ordered(join_kernel, 1 + len(arrays), deps),
        [((before, len(arrays), units, width), kind)],
        name,
        in_specs=[pl.BlockSpec(memory_space=pltpu.SMEM)]
        + [pl.BlockSpec(memory_space=pltpu.VMEM)] * len(arrays)
        + unread(deps),
    )(at, *arrays, *deps)
    return out


def join_last_kernel(_, piece, *refs):
    refs[-1][:, 0] = piece[...].astype(F32)


def join_last(at, piece, filled, name):
    before, units, width = piece.shape
    step = max(1, before // 4)
    return pl.pallas_call(
        join_last_kernel,
        grid_spec=pltpu.PrefetchScalarGridSpec(
            num_scalar_prefetch=1,
            grid=(before // step,),
            in_specs=[pl.BlockSpec((step, units, width), lambda g, at: (g, 0, 0))] + unread(filled),
            out_specs=pl.BlockSpec((step, 1, units, width), lambda g, at: (g, at[0], 0, 0)),
        ),
        out_shape=pltpu.HBM((before, 2, units, width), F32),
        input_output_aliases={2: 0} if filled else {},
        compiler_params=params(),
        name=name,
    )(at, piece, *filled)


def tail_kernel(
    upstream, inter, gain, crossed, mixing, grad_top, partial, proj_y, proj_p, slot_col, *refs
):
    out, place = refs[-2:]
    owners, _, slots, width = out.shape
    fields = owners * slots
    made = mixing.shape[1]

    @pl.when(pl.program_id(0) == 0)
    def _():
        field = lax.broadcasted_iota(jnp.int32, (fields, fields), 1)
        place[...] = jnp.where(field == slot_col[...], 1.0, 0.0).astype(BF)

    unit, scale = layer_norm(inter[...])
    grad_inter = norm_back(unit, scale, gain[...], upstream[...]).astype(BF)
    grad_mixing = nt(grad_inter, crossed[0]).astype(BF)
    grad_crossed = tn(mixing[0], grad_inter).astype(BF)
    grad = partial[0] + tn(proj_p[...], grad_mixing) + nt(proj_y[...], grad_crossed)
    head = (grad[:made] + grad_top[...]).astype(BF)
    grad = jnp.concatenate([head, grad[made:].astype(BF)], axis=0)
    out[:, 0] = nn(place[...], grad).astype(BF).reshape(owners, slots, width)


def tail(upstream, kept, gain, proj_y, proj_p, slot_field, owners, deps):
    inter, crossed, mixing, grad_top, partial = kept
    samples, fields, width = partial.shape
    rank = proj_y.shape[1]
    made = mixing.shape[1]
    slots = fields // owners
    return pl.pallas_call(
        ordered(tail_kernel, 10, deps),
        grid=(samples,),
        in_specs=[
            by_sample(made, rank),
            by_sample(made, rank),
            const(1, rank),
            by_sample(1, width, rank),
            by_sample(1, made, width),
            by_sample(made, width),
            by_sample(1, fields, width),
            const(fields, rank),
            const(made, fields),
            const(fields, 1),
        ]
        + unread(deps),
        out_specs=pl.BlockSpec((owners, 1, slots, width), lambda b: (0, b, 0, 0)),
        out_shape=jax.ShapeDtypeStruct((owners, samples, slots, width), BF),
        scratch_shapes=[pltpu.VMEM((fields, fields), BF)],
        compiler_params=params(),
        name="tail",
    )(
        upstream,
        inter,
        gain,
        crossed,
        mixing,
        grad_top,
        partial,
        proj_y,
        proj_p,
        slot_field[:, None],
        *deps,
    )


def whole(kernel, shapes, name, **options):
    return pl.pallas_call(
        kernel,
        out_shape=[jax.ShapeDtypeStruct(shape, kind) for shape, kind in shapes],
        compiler_params=params(),
        name=name,
        **options,
    )


def turn(value, axis, size, shift):
    return lax.ppermute(value, axis, [(i, (i + shift) % size) for i in range(size)])


def after(value, *others):
    return lax.optimization_barrier((value, *others))[0]


def body(
    sizes,
    tables,
    bag_ids,
    bag_lengths,
    slot_field,
    proj_y,
    proj_p,
    linear_w,
    fm_gain,
    w_up,
    w_down,
    out_gain,
    cotangent,
):
    wide = sizes["wide"]
    emb = tuple(axis for axis in sizes if axis != "wide")
    owners = 2 ** len(emb)
    width = tables.shape[2]
    made = proj_p.shape[0]
    cot = cotangent[0]
    samples = cot.shape[0]
    gain_fm, gain_out = fm_gain[None, :], out_gain[None, :]
    places = {axis: lax.axis_index(axis).astype(jnp.int32)[None] for axis in emb}

    *outer, mid, near = emb

    def spread(value):
        return [turn(value, "wide", wide, k) for k in range(1, wide)]

    def exchange(value):
        flat = value.reshape(owners * samples, *value.shape[2:])
        moved = lax.all_to_all(flat, emb, split_axis=0, concat_axis=0, tiled=True)
        return moved.reshape(value.shape)

    fetched = spread(lax.select(places[near][0] == 0, w_up, w_down))
    (pooled,) = pool_bags(tables, bag_ids[0], bag_lengths[0], owners, 1)
    received = exchange(pooled)
    embeds, crossed, mixing, inter, rows = front(
        received, slot_field, proj_y, proj_p, gain_fm, [], samples, 0, [], "front"
    )
    all_rows = [rows, *spread(rows)]
    ff = mlp(up_kernel, places[near], [rows], w_up, w_down, [], [], None, [], "up_own")
    fetched, _ = lax.optimization_barrier((fetched, rows))
    traded = [turn(weight, near, 2, 1) for weight in fetched]
    ff = mlp(up_kernel, places[near], [rows], w_up, w_down, fetched, traded, ff, [], "up_other", False)
    layer_out, grad_top, grads = top(ff, embeds, gain_out, cot)
    all_grads = [grads, *spread(grads)]
    layer_out, partial = linear(embeds, linear_w, gain_out, cot, layer_out, [grads])

    units = w_up.shape[0] // owners
    shared = (owners // 2, 2, units, width)
    shares = (w_up.reshape(shared), w_down.reshape(shared))
    away = weight_grads(1 - places[near], all_rows, all_grads, *shares, BF, [partial], "weights_1")
    arrived = [turn(part, near, 2, 1) for part in away]
    kept_parts = weight_grads(places[near], all_rows, all_grads, *shares, F32, [away[0]], "weights_0")
    last = [kept_parts[0]]
    sums = [list(terms) for terms in zip(kept_parts, arrived)]

    def cut(arrays, size):
        return [a.reshape(-1, size, units, width) for a in arrays]

    def halve(n, axis):
        nonlocal last
        name = f"{('down', 'up')[n]}_split_{axis}"
        ((keep, away),) = split_sum(places[axis], 2, [cut(sums[n], 2)], F32, last, name)
        last = [away]
        sums[n] = [keep, turn(away, axis, 2, 1)]

    halve(0, mid)
    halve(1, mid)
    upstream = mlp(back_kernel, places[near], [rows, grads], w_up, w_down, fetched, traded, None, last, "back")
    last = [upstream]
    halve(0, outer[-1])
    slot_grads = tail(
        upstream,
        (inter, crossed, mixing, grad_top, partial),
        gain_fm,
        proj_y,
        proj_p,
        slot_field,
        owners,
        last,
    )
    last = [slot_grads]
    halve(1, outer[-1])
    returned = exchange(slot_grads)
    for axis in reversed(outer[:-1]):
        halve(0, axis)
        halve(1, axis)
    weights, orders = [], []
    for n, name in enumerate(("down", "up")):
        ((share,),) = split_sum(places[near], 1, [cut(sums[n], 1)], BF, last, f"{name}_share")
        last = [share]
        weights.append(share.reshape(-1, width))
        orders.append((*outer, mid, near) if n == 0 else (*outer[:1], mid, *outer[1:], near))
    done = [[], []]
    for step in range(len(emb)):
        for n, name in enumerate(("down", "up")):
            axis = orders[n][step]
            at = emb.index(axis)
            before = 2 ** sum(emb.index(other) < at for other in done[n])
            value = weights[n].reshape(before, -1, width)
            other = turn(value, axis, 2, 1)
            if step == len(emb) - 1:
                joined = join_last(places[axis], value, [], f"{name}_keep_{axis}")
                joined = join_last(1 - places[axis], other, [joined], f"{name}_join_{axis}")
            else:
                joined = join(places[axis], [value, other], BF, last, f"{name}_join_{axis}")
                last = [joined]
            weights[n] = joined.reshape(-1, width)
            done[n].append(axis)
    down, up = [w.reshape(-1, width) for w in weights]
    return (layer_out[None], returned.reshape(1, owners * samples, -1, width), up, down)


def solution(mesh):
    emb, wide = mesh.shape["emb"], mesh.shape["wide"]
    names = tuple(f"emb_{k}" for k in range(emb.bit_length() - 1))
    split = Mesh(mesh.devices.reshape((2,) * len(names) + (wide,)), (*names, "wide"))
    return jax.shard_map(
        functools.partial(body, dict(split.shape)),
        mesh=split,
        in_specs=(
            P(names, None, None),
            P("wide", None, names, None),
            P("wide", None, names),
            P(),
            P(),
            P(),
            P(),
            P(),
            P("wide", None),
            P("wide", None),
            P(),
            P("wide", names, None, None),
        ),
        out_specs=(
            P("wide", names, None, None),
            P("wide", None, names, None),
            P("wide", None),
            P("wide", None),
        ),
        check_vma=False,
    )
```

```python
import functools

import jax
import jax.numpy as jnp
from jax import lax
from jax.experimental import pallas as pl
from jax.experimental.pallas import tpu as pltpu
from jax.sharding import Mesh
from jax.sharding import PartitionSpec as P

norm_eps = 1e-05
VMEM_BYTES = 24 * 1024 * 1024
BF = jnp.bfloat16
F32 = jnp.float32
WIDE_BYTES = 56 * 1024 * 1024
LANES = 128
PART = 256


def params(limit=VMEM_BYTES):
    return pltpu.CompilerParams(vmem_limit_bytes=limit)


def ordered(kernel, ins, deps):
    return lambda *refs: kernel(*refs[:ins], *refs[ins + len(deps) :])


def unread(deps):
    return [pl.BlockSpec(memory_space=pl.ANY)] * len(deps)


def nn(left, right):
    return lax.dot_general(left, right, (((1,), (0,)), ((), ())), preferred_element_type=F32)


def nt(left, right):
    return lax.dot_general(left, right, (((1,), (1,)), ((), ())), preferred_element_type=F32)


def tn(left, right):
    return lax.dot_general(left, right, (((0,), (0,)), ((), ())), preferred_element_type=F32)


def layer_norm(values):
    centre = jnp.mean(values, axis=-1, keepdims=True)
    shifted = values - centre
    scale = lax.rsqrt(jnp.mean(shifted * shifted, axis=-1, keepdims=True) + norm_eps)
    return (shifted * scale, scale)


def norm_back(unit, scale, gain, upstream):
    scaled = upstream * gain
    return scale * (
        scaled
        - jnp.mean(scaled, axis=-1, keepdims=True)
        - unit * jnp.mean(scaled * unit, axis=-1, keepdims=True)
    )


def pool_kernel(ids_ref, tables_ref, *refs):
    outs, sums = refs[:-1], refs[-1]
    slots, samples, bag = ids_ref.shape
    buckets = tables_ref.shape[1]
    here = outs[0].shape[1]
    bucket = lax.broadcasted_iota(jnp.int32, (samples, buckets), 1)
    for s in range(slots):
        ids = ids_ref[s]
        count = jnp.zeros((samples, buckets), F32)
        for j in range(bag):
            count = count + jnp.where(ids[:, j : j + 1] == bucket, 1.0, 0.0)
        bags = nn(count.astype(BF), tables_ref[s])
        for c in range(sums.shape[0]):
            sums[c, pl.ds(s * samples, samples), :] = bags[:, c * LANES : (c + 1) * LANES]
    for b in range(samples):
        owner, local = divmod(b, here * len(outs))
        out = outs[local // here]
        for c in range(sums.shape[0]):
            bag_sums = sums.at[c][pl.ds(b, slots, stride=samples), :]
            out[owner, local % here, :, c * LANES : (c + 1) * LANES] = bag_sums.astype(BF)


def pool_bags(tables, ids, lengths, owners, halves):
    slots, buckets, width = tables.shape
    samples, _, bag = ids.shape
    here = samples // owners // halves
    live = jnp.arange(bag, dtype=jnp.int32)[None, None, :] < lengths[:, :, None]
    masked = jnp.where(live, ids, -1).transpose(1, 0, 2)
    step = 16 if slots % 16 == 0 else slots
    return pl.pallas_call(
        pool_kernel,
        grid=(slots // step,),
        in_specs=[
            pl.BlockSpec((step, samples, bag), lambda g: (g, 0, 0)),
            pl.BlockSpec((step, buckets, width), lambda g: (g, 0, 0)),
        ],
        out_specs=[pl.BlockSpec((owners, here, step, width), lambda g: (0, 0, g, 0))] * halves,
        out_shape=[jax.ShapeDtypeStruct((owners, here, slots, width), BF)] * halves,
        scratch_shapes=[pltpu.VMEM((width // LANES, step * samples, LANES), F32)],
        compiler_params=params(),
        name="pool",
    )(masked, tables)


def const(*shape):
    return pl.BlockSpec(shape, lambda *_: (0,) * len(shape))


def by_sample(*shape):
    return pl.BlockSpec(shape, lambda b: (b,) + (0,) * (len(shape) - 1))


def from_sample(start, *shape):
    return pl.BlockSpec(shape, lambda b: (start + b,) + (0,) * (len(shape) - 1))


def front_kernel(rec, slot_row, proj_y, proj_p, gain, *refs):
    embeds, crossed, mixing, inter, rows, place = refs[-6:]
    owners, _, slots, width = rec.shape
    fields = owners * slots

    @pl.when(pl.program_id(0) == 0)
    def _():
        field = lax.broadcasted_iota(jnp.int32, (fields, fields), 0)
        place[...] = jnp.where(field == slot_row[...], 1.0, 0.0).astype(BF)

    x = nn(place[...], rec[:, 0].reshape(fields, width)).astype(BF)
    embeds[0] = x
    c = tn(x, proj_y[...]).astype(BF)
    crossed[0] = c
    m = nn(proj_p[...], x).astype(BF)
    mixing[0] = m
    v = nn(m, c)
    inter[...] = v
    unit, _ = layer_norm(v)
    rows[...] = (unit * gain[...]).astype(BF)


def front(received, slot_field, proj_y, proj_p, gain, filled, samples, start, deps, name):
    owners, here, slots, width = received.shape
    fields, rank = proj_y.shape
    made = proj_p.shape[0]
    return pl.pallas_call(
        ordered(front_kernel, 5 + len(filled), deps),
        grid=(here,),
        in_specs=[
            pl.BlockSpec((owners, 1, slots, width), lambda b: (0, b, 0, 0)),
            const(1, fields),
            const(fields, rank),
            const(made, fields),
            const(1, rank),
        ]
        + unread(filled)
        + unread(deps),
        out_specs=[
            by_sample(1, fields, width),
            from_sample(start, 1, width, rank),
            from_sample(start, 1, made, width),
            from_sample(start, made, rank),
            by_sample(made, rank),
        ],
        out_shape=[
            jax.ShapeDtypeStruct((here, fields, width), BF),
            pltpu.HBM((samples, width, rank), BF),
            pltpu.HBM((samples, made, width), BF),
            pltpu.HBM((samples * made, rank), F32),
            jax.ShapeDtypeStruct((here * made, rank), BF),
        ],
        input_output_aliases={5: 1, 6: 2, 7: 3} if filled else {},
        scratch_shapes=[pltpu.VMEM((fields, fields), BF)],
        compiler_params=params(),
        name=name,
    )(received, slot_field[None, :], proj_y, proj_p, gain, *filled, *deps)


def linear_kernel(embeds, linear_w, gain, cot, layer_out, partial):
    made = linear_w.shape[0]
    first = embeds.shape[1] - made
    x = embeds[0]
    summed = nn(linear_w[...], x) + x[first:].astype(F32)
    unit, scale = layer_norm(summed)
    layer_out[0, :first] = jnp.zeros_like(layer_out[0, :first])
    layer_out[0, first:] = (unit * gain[...]).astype(BF)
    grad = norm_back(unit, scale, gain[...], cot[0, first:].astype(F32))
    back = tn(linear_w[...], grad.astype(BF))
    partial[0, :first] = back[:first]
    partial[0, first:] = back[first:] + grad


def linear(embeds, linear_w, gain, cot, deps):
    samples, fields, width = embeds.shape
    return pl.pallas_call(
        ordered(linear_kernel, 4, deps),
        grid=(samples,),
        in_specs=[
            by_sample(1, fields, width),
            const(*linear_w.shape),
            const(1, width),
            by_sample(1, fields, width),
        ]
        + unread(deps),
        out_specs=[by_sample(1, fields, width)] * 2,
        out_shape=[pltpu.HBM(cot.shape, BF), pltpu.HBM(cot.shape, F32)],
        compiler_params=params(),
        name="linear",
    )(embeds, linear_w, gain, cot, *deps)


def activate(gate):
    sig = 0.5 * jnp.tanh(0.5 * gate) + 0.5
    h = gate * sig
    return (h.astype(BF), sig + h * (1.0 - sig))


def tiles_of(weight, others, own, most):
    units, width = weight.shape
    tile = min(most, units)
    steps = units // tile
    specs = [
        pl.BlockSpec(
            (tile, width), lambda g, at, n=n: (jnp.clip(g - n * steps, 0, steps - 1), 0)
        )
        for n in range(own + len(others))
    ]
    return steps, specs


def at_tiles(steps, own, near, refs, work):
    step = pl.program_id(0)
    count = len(refs) // 2 - own

    if own:

        @pl.when(step < steps)
        def _():
            work(refs[0], refs[1])

    for n in range(count):
        fetched, traded = refs[2 * own + n], refs[2 * own + count + n]
        here = jnp.logical_and(step >= (n + own) * steps, step < (n + own + 1) * steps)

        @pl.when(jnp.logical_and(here, near[0] == 0))
        def _(up=fetched, down=traded):
            work(up, down)

        @pl.when(jnp.logical_and(here, near[0] != 0))
        def _(up=traded, down=fetched):
            work(up, down)


def accumulate(out, begun, term):
    @pl.when(pl.program_id(0) == 0)
    def _():
        out[...] = term if begun is None else begun[...] + term

    @pl.when(pl.program_id(0) > 0)
    def _():
        out[...] += term


def up_kernel(steps, own, begun, near, rows, *refs):
    def work(up, down):
        hidden, _ = activate(nt(rows[...], up[...]))
        accumulate(refs[-1], refs[0] if begun else None, nn(hidden, down[...]))

    at_tiles(steps, own, near, refs[begun:-1], work)


def back_kernel(steps, own, begun, near, rows, grads, *refs):
    def work(up, down):
        term = None
        gate, grad = nt(rows[...], up[:PART, :]), nt(grads[...], down[:PART, :])
        for at in range(0, up.shape[0], PART):
            now, grad_now, after = gate, grad, at + PART
            if after < up.shape[0]:
                gate = nt(rows[...], up[after : after + PART, :])
                grad = nt(grads[...], down[after : after + PART, :])
            _, slope = activate(now)
            more = nn((grad_now * slope).astype(BF), up[at:after, :])
            term = more if term is None else term + more
        accumulate(refs[-1], refs[0] if begun else None, term)

    at_tiles(steps, own, near, refs[begun:-1], work)


def mlp(kernel, near, blocks, w_up, w_down, fetched, traded, begun, deps, name, own=True, limit=VMEM_BYTES):
    steps, specs = tiles_of(w_up, fetched, own, 1024)
    begun = [] if begun is None else [begun]
    weights = [w_up, w_down] if own else []
    ins = 1 + len(blocks) + len(begun) + len(weights) + 2 * len(fetched)
    return pl.pallas_call(
        ordered(functools.partial(kernel, steps, int(own), len(begun)), ins, deps),
        grid_spec=pltpu.PrefetchScalarGridSpec(
            num_scalar_prefetch=1,
            grid=(steps * len(specs),),
            in_specs=[const(*block.shape) for block in (*blocks, *begun)]
            + specs[:own] * 2
            + specs[own:] * 2
            + unread(deps),
            out_specs=const(*blocks[0].shape),
        ),
        out_shape=jax.ShapeDtypeStruct(blocks[0].shape, F32),
        compiler_params=params(limit),
        name=name,
    )(near, *blocks, *begun, *weights, *fetched, *traded, *deps)


def top_kernel(ff, embeds, gain, cot, _, layer_out, grad, grad_ff):
    summed = ff[...] + embeds[0].astype(F32)
    unit, scale = layer_norm(summed)
    layer_out[0] = (unit * gain[...]).astype(BF)
    g = norm_back(unit, scale, gain[...], cot[0].astype(F32))
    grad[...] = g
    grad_ff[...] = g.astype(BF)


def top(ff, embeds, gain, cot, layer_out):
    samples, _, width = embeds.shape
    made = ff.shape[0] // samples
    return pl.pallas_call(
        top_kernel,
        grid=(samples,),
        in_specs=[
            by_sample(made, width),
            by_sample(1, made, width),
            const(1, width),
            by_sample(1, made, width),
        ]
        + unread([layer_out]),
        out_specs=[by_sample(1, made, width), by_sample(made, width), by_sample(made, width)],
        out_shape=[
            pltpu.HBM(cot.shape, BF),
            jax.ShapeDtypeStruct(ff.shape, F32),
            jax.ShapeDtypeStruct(ff.shape, BF),
        ],
        input_output_aliases={4: 0},
        compiler_params=params(),
        name="top",
    )(ff, embeds, gain, cot, layer_out)


def fill(blocks, out):
    at = 0
    for block in blocks:
        out[at : at + block.shape[0]] = block[...]
        at += block.shape[0]


def weight_kernel(blocks, _, *refs):
    w_up, w_down, grad_down, grad_up, rows, grads = refs[2 * blocks :]

    @pl.when(pl.program_id(0) == 0)
    def _():
        fill(refs[:blocks], rows)
        fill(refs[blocks : 2 * blocks], grads)

    shares, units, width = grad_down.shape
    up = w_up[...].reshape(shares * units, width)
    down = w_down[...].reshape(shares * units, width)
    hidden, slope = activate(nt(up, rows[...]))
    gated = (nt(down, grads[...]) * slope).astype(BF)
    for out, left, right in ((grad_down, hidden, grads), (grad_up, gated, rows)):
        out[...] = nn(left, right[...]).reshape(shares, units, width).astype(out.dtype)


def weight_grads(at, rows, grads, w_up, w_down, kind, deps, name):
    shares, _, units, width = w_up.shape
    blocks = len(rows)
    count = sum(block.shape[0] for block in rows)
    step = max(1, min(shares, 1024 // units if count <= 1024 else 128 // units))
    shared = pl.BlockSpec((step, 1, units, width), lambda g, at: (g, at[0], 0, 0))
    given = pl.BlockSpec((step, units, width), lambda g, at: (g, 0, 0))
    return pl.pallas_call(
        ordered(functools.partial(weight_kernel, blocks), 1 + 2 * blocks + 2, deps),
        grid_spec=pltpu.PrefetchScalarGridSpec(
            num_scalar_prefetch=1,
            grid=(shares // step,),
            in_specs=[const(*block.shape) for block in (*rows, *grads)]
            + [shared, shared]
            + unread(deps),
            out_specs=[given, given],
            scratch_shapes=[pltpu.VMEM((count, width), BF)] * 2,
        ),
        out_shape=[jax.ShapeDtypeStruct((shares, units, width), kind)] * 2,
        compiler_params=params(WIDE_BYTES),
        name=name,
    )(at, *rows, *grads, w_up, w_down, *deps)


def split_kernel(count, each, at, *refs):
    ins, outs = refs[: -count * len(each)], refs[-count * len(each) :]
    for k in reversed(range(count)):
        here = lax.rem(at[0] + k, count)
        first = 0
        for n, terms in enumerate(each):
            total = ins[first][:, here].astype(F32)
            for ref in ins[first + 1 : first + terms]:
                total = total + ref[:, here].astype(F32)
            out = outs[n * count + k]
            out[...] = total.astype(out.dtype)
            first += terms


def split_sum(at, count, sums, kind, deps, name):
    outs = []
    for arrays in sums:
        before, _, units, width = arrays[0].shape
        outs += [((before, units, width), kind if k == 0 else BF) for k in range(count)]
    each = [len(arrays) for arrays in sums]
    pieces = whole(
        ordered(functools.partial(split_kernel, count, each), 1 + sum(each), deps),
        outs,
        name,
        in_specs=[pl.BlockSpec(memory_space=pltpu.SMEM)]
        + [pl.BlockSpec(memory_space=pltpu.VMEM)] * sum(each)
        + unread(deps),
    )(at, *[array for arrays in sums for array in arrays], *deps)
    return [pieces[n * count : (n + 1) * count] for n in range(len(sums))]


def join_kernel(at, *refs):
    ins, out = refs[:-1], refs[-1]
    count = len(ins)
    for k, ref in enumerate(ins):
        out[:, lax.rem(at[0] + (count - k), count)] = ref[...].astype(out.dtype)


def join(at, arrays, kind, deps, name):
    before, units, width = arrays[0].shape
    (out,) = whole(
        ordered(join_kernel, 1 + len(arrays), deps),
        [((before, len(arrays), units, width), kind)],
        name,
        in_specs=[pl.BlockSpec(memory_space=pltpu.SMEM)]
        + [pl.BlockSpec(memory_space=pltpu.VMEM)] * len(arrays)
        + unread(deps),
    )(at, *arrays, *deps)
    return out


def join_last_kernel(count, _, *refs):
    for piece, out in zip(refs[:count], refs[-count:]):
        out[:, 0] = piece[...].astype(F32)


def join_last(at, pieces, filled, name):
    before, units, width = pieces[0].shape
    count = len(pieces)
    step = max(1, before // 4)
    return pl.pallas_call(
        functools.partial(join_last_kernel, count),
        grid_spec=pltpu.PrefetchScalarGridSpec(
            num_scalar_prefetch=1,
            grid=(before // step,),
            in_specs=[pl.BlockSpec((step, units, width), lambda g, at: (g, 0, 0))] * count
            + unread(filled),
            out_specs=[pl.BlockSpec((step, 1, units, width), lambda g, at: (g, at[0], 0, 0))] * count,
        ),
        out_shape=[pltpu.HBM((before, 2, units, width), F32)] * count,
        input_output_aliases={1 + count + n: n for n in range(len(filled))},
        compiler_params=params(),
        name=name,
    )(at, *pieces, *filled)


def tail_kernel(
    upstream, inter, gain, crossed, mixing, grad_top, partial, proj_y, proj_p, slot_col, *refs
):
    out, place = refs[-2:]
    owners, _, slots, width = out.shape
    fields = owners * slots
    made = mixing.shape[1]

    @pl.when(pl.program_id(0) == 0)
    def _():
        field = lax.broadcasted_iota(jnp.int32, (fields, fields), 1)
        place[...] = jnp.where(field == slot_col[...], 1.0, 0.0).astype(BF)

    unit, scale = layer_norm(inter[...])
    grad_inter = norm_back(unit, scale, gain[...], upstream[...]).astype(BF)
    grad_mixing = nt(grad_inter, crossed[0]).astype(BF)
    grad_crossed = tn(mixing[0], grad_inter).astype(BF)
    grad = partial[0] + tn(proj_p[...], grad_mixing) + nt(proj_y[...], grad_crossed)
    head = (grad[:made] + grad_top[...]).astype(BF)
    grad = jnp.concatenate([head, grad[made:].astype(BF)], axis=0)
    out[:, 0] = nn(place[...], grad).astype(BF).reshape(owners, slots, width)


def tail(upstream, kept, gain, proj_y, proj_p, slot_field, owners, deps):
    inter, crossed, mixing, grad_top, partial = kept
    samples, fields, width = partial.shape
    rank = proj_y.shape[1]
    made = mixing.shape[1]
    slots = fields // owners
    return pl.pallas_call(
        ordered(tail_kernel, 10, deps),
        grid=(samples,),
        in_specs=[
            by_sample(made, rank),
            by_sample(made, rank),
            const(1, rank),
            by_sample(1, width, rank),
            by_sample(1, made, width),
            by_sample(made, width),
            by_sample(1, fields, width),
            const(fields, rank),
            const(made, fields),
            const(fields, 1),
        ]
        + unread(deps),
        out_specs=pl.BlockSpec((owners, 1, slots, width), lambda b: (0, b, 0, 0)),
        out_shape=jax.ShapeDtypeStruct((owners, samples, slots, width), BF),
        scratch_shapes=[pltpu.VMEM((fields, fields), BF)],
        compiler_params=params(),
        name="tail",
    )(
        upstream,
        inter,
        gain,
        crossed,
        mixing,
        grad_top,
        partial,
        proj_y,
        proj_p,
        slot_field[:, None],
        *deps,
    )


def whole(kernel, shapes, name, **options):
    return pl.pallas_call(
        kernel,
        out_shape=[jax.ShapeDtypeStruct(shape, kind) for shape, kind in shapes],
        compiler_params=params(),
        name=name,
        **options,
    )


def turn(value, axis, size, shift):
    return lax.ppermute(value, axis, [(i, (i + shift) % size) for i in range(size)])


def after(value, *others):
    return lax.optimization_barrier((value, *others))[0]


def body(
    sizes,
    tables,
    bag_ids,
    bag_lengths,
    slot_field,
    proj_y,
    proj_p,
    linear_w,
    fm_gain,
    w_up,
    w_down,
    out_gain,
    cotangent,
):
    wide = sizes["wide"]
    emb = tuple(axis for axis in sizes if axis != "wide")
    owners = 2 ** len(emb)
    width = tables.shape[2]
    made = proj_p.shape[0]
    cot = cotangent[0]
    samples = cot.shape[0]
    gain_fm, gain_out = fm_gain[None, :], out_gain[None, :]
    places = {axis: lax.axis_index(axis).astype(jnp.int32)[None] for axis in emb}

    *outer, mid, near = emb

    def spread(value):
        return [turn(value, "wide", wide, k) for k in range(1, wide)]

    def exchange(value):
        flat = value.reshape(owners * samples, *value.shape[2:])
        moved = lax.all_to_all(flat, emb, split_axis=0, concat_axis=0, tiled=True)
        return moved.reshape(value.shape)

    fetched = spread(lax.select(places[near][0] == 0, w_up, w_down))
    (pooled,) = pool_bags(tables, bag_ids[0], bag_lengths[0], owners, 1)
    received = exchange(pooled)
    embeds, crossed, mixing, inter, rows = front(
        received, slot_field, proj_y, proj_p, gain_fm, [], samples, 0, [], "front"
    )
    all_rows = [rows, *spread(rows)]
    fetched, _ = lax.optimization_barrier((fetched, rows))
    traded = [turn(weight, near, 2, 1) for weight in fetched]
    layer_out, partial = linear(embeds, linear_w, gain_out, cot, [rows])
    ff = mlp(up_kernel, places[near], [rows], w_up, w_down, [], [], None, [partial], "up_own")
    ff = mlp(up_kernel, places[near], [rows], w_up, w_down, fetched, traded, ff, [], "up_other", False)
    layer_out, grad_top, grads = top(ff, embeds, gain_out, cot, layer_out)
    all_grads = [grads, *spread(grads)]

    units = w_up.shape[0] // owners
    shared = (owners // 2, 2, units, width)
    shares = (w_up.reshape(shared), w_down.reshape(shared))
    upstream = mlp(
        back_kernel,
        places[near],
        [rows, grads],
        w_up,
        w_down,
        fetched,
        traded,
        None,
        [],
        "back",
        limit=WIDE_BYTES,
    )
    slot_grads = tail(
        upstream,
        (inter, crossed, mixing, grad_top, partial),
        gain_fm,
        proj_y,
        proj_p,
        slot_field,
        owners,
        [*all_rows[1:], *all_grads[1:]],
    )
    returned = exchange(slot_grads)
    away = weight_grads(1 - places[near], all_rows, all_grads, *shares, BF, [slot_grads], "weights_1")
    arrived = [turn(part, near, 2, 1) for part in away]
    kept_parts = weight_grads(places[near], all_rows, all_grads, *shares, BF, [away[0]], "weights_0")
    last = [kept_parts[0]]
    sums = [list(terms) for terms in zip(kept_parts, arrived)]

    orders = [(*outer, mid, near), (*outer[:1], mid, *outer[1:], near)]
    left = [list(emb[:-1]), list(emb[:-1])]

    def halve(n, step):
        nonlocal last
        axis = orders[n][step]
        before = 2 ** left[n].index(axis)
        left[n].remove(axis)
        terms = [term.reshape(before, 2, -1, width) for term in sums[n]]
        name = f"{('down', 'up')[n]}_split_{axis}"
        ((keep, away),) = split_sum(places[axis], 2, [terms], F32, last, name)
        last = [away]
        sums[n] = [keep, turn(away, axis, 2, 1)]

    for step in range(len(emb) - 2, -1, -1):
        halve(0, step)
        halve(1, step)
        if step == len(emb) - 2:
            last = [*last, returned]
    weights = []
    for n, name in enumerate(("down", "up")):
        terms = [term.reshape(1, 1, units, width) for term in sums[n]]
        ((share,),) = split_sum(places[near], 1, [terms], BF, last, f"{name}_share")
        last = [share]
        weights.append(share.reshape(-1, width))
    done = [[], []]
    for step in range(len(emb) - 1):
        for n, name in enumerate(("down", "up")):
            axis = orders[n][step]
            at = emb.index(axis)
            before = 2 ** sum(emb.index(other) < at for other in done[n])
            value = weights[n].reshape(before, -1, width)
            other = turn(value, axis, 2, 1)
            joined = join(places[axis], [value, other], BF, last, f"{name}_join_{axis}")
            last = [joined]
            weights[n] = joined.reshape(-1, width)
            done[n].append(axis)
    mine = [value.reshape(owners // 2, units, width) for value in weights]
    others = [turn(value, near, 2, 1) for value in mine]
    joined = join_last(places[near], mine, [], "weights_mine")
    joined = join_last(1 - places[near], others, joined, "weights_others")
    down, up = [value.reshape(-1, width) for value in joined]
    return (layer_out[None], returned.reshape(1, owners * samples, -1, width), up, down)


def solution(mesh):
    emb, wide = mesh.shape["emb"], mesh.shape["wide"]
    names = tuple(f"emb_{k}" for k in range(emb.bit_length() - 1))
    split = Mesh(mesh.devices.reshape((2,) * len(names) + (wide,)), (*names, "wide"))
    return jax.shard_map(
        functools.partial(body, dict(split.shape)),
        mesh=split,
        in_specs=(
            P(names, None, None),
            P("wide", None, names, None),
            P("wide", None, names),
            P(),
            P(),
            P(),
            P(),
            P(),
            P("wide", None),
            P("wide", None),
            P(),
            P("wide", names, None, None),
        ),
        out_specs=(
            P("wide", names, None, None),
            P("wide", None, names, None),
            P("wide", None),
            P("wide", None),
        ),
        check_vma=False,
    )
```

```python
import functools

import jax
import jax.numpy as jnp
from jax import lax
from jax.experimental import pallas as pl
from jax.experimental.pallas import tpu as pltpu
from jax.sharding import Mesh
from jax.sharding import PartitionSpec as P

norm_eps = 1e-05
VMEM_BYTES = 24 * 1024 * 1024
BF = jnp.bfloat16
F32 = jnp.float32
WIDE_BYTES = 56 * 1024 * 1024
LANES = 128
PART = 256


def params(limit=VMEM_BYTES):
    return pltpu.CompilerParams(vmem_limit_bytes=limit)


def ordered(kernel, ins, deps):
    return lambda *refs: kernel(*refs[:ins], *refs[ins + len(deps) :])


def unread(deps):
    return [pl.BlockSpec(memory_space=pl.ANY)] * len(deps)


def nn(left, right):
    return lax.dot_general(left, right, (((1,), (0,)), ((), ())), preferred_element_type=F32)


def nt(left, right):
    return lax.dot_general(left, right, (((1,), (1,)), ((), ())), preferred_element_type=F32)


def tn(left, right):
    return lax.dot_general(left, right, (((0,), (0,)), ((), ())), preferred_element_type=F32)


def layer_norm(values):
    centre = jnp.mean(values, axis=-1, keepdims=True)
    shifted = values - centre
    scale = lax.rsqrt(jnp.mean(shifted * shifted, axis=-1, keepdims=True) + norm_eps)
    return (shifted * scale, scale)


def norm_back(unit, scale, gain, upstream):
    scaled = upstream * gain
    return scale * (
        scaled
        - jnp.mean(scaled, axis=-1, keepdims=True)
        - unit * jnp.mean(scaled * unit, axis=-1, keepdims=True)
    )


def pool_kernel(ids_ref, tables_ref, *refs):
    outs, sums = refs[:-1], refs[-1]
    slots, samples, bag = ids_ref.shape
    buckets = tables_ref.shape[1]
    here = outs[0].shape[1]
    bucket = lax.broadcasted_iota(jnp.int32, (samples, buckets), 1)
    for s in range(slots):
        ids = ids_ref[s]
        count = jnp.zeros((samples, buckets), F32)
        for j in range(bag):
            count = count + jnp.where(ids[:, j : j + 1] == bucket, 1.0, 0.0)
        bags = nn(count.astype(BF), tables_ref[s])
        for c in range(sums.shape[0]):
            sums[c, pl.ds(s * samples, samples), :] = bags[:, c * LANES : (c + 1) * LANES]
    for b in range(samples):
        owner, local = divmod(b, here * len(outs))
        out = outs[local // here]
        for c in range(sums.shape[0]):
            bag_sums = sums.at[c][pl.ds(b, slots, stride=samples), :]
            out[owner, local % here, :, c * LANES : (c + 1) * LANES] = bag_sums.astype(BF)


def pool_bags(tables, ids, lengths, owners, halves):
    slots, buckets, width = tables.shape
    samples, _, bag = ids.shape
    here = samples // owners // halves
    live = jnp.arange(bag, dtype=jnp.int32)[None, None, :] < lengths[:, :, None]
    masked = jnp.where(live, ids, -1).transpose(1, 0, 2)
    step = 16 if slots % 16 == 0 else slots
    return pl.pallas_call(
        pool_kernel,
        grid=(slots // step,),
        in_specs=[
            pl.BlockSpec((step, samples, bag), lambda g: (g, 0, 0)),
            pl.BlockSpec((step, buckets, width), lambda g: (g, 0, 0)),
        ],
        out_specs=[pl.BlockSpec((owners, here, step, width), lambda g: (0, 0, g, 0))] * halves,
        out_shape=[jax.ShapeDtypeStruct((owners, here, slots, width), BF)] * halves,
        scratch_shapes=[pltpu.VMEM((width // LANES, step * samples, LANES), F32)],
        compiler_params=params(),
        name="pool",
    )(masked, tables)


def const(*shape):
    return pl.BlockSpec(shape, lambda *_: (0,) * len(shape))


def by_sample(*shape):
    return pl.BlockSpec(shape, lambda b: (b,) + (0,) * (len(shape) - 1))


def from_sample(start, *shape):
    return pl.BlockSpec(shape, lambda b: (start + b,) + (0,) * (len(shape) - 1))


def front_kernel(rec, slot_row, proj_y, proj_p, gain, *refs):
    embeds, crossed, mixing, inter, rows, place = refs[-6:]
    owners, _, slots, width = rec.shape
    fields = owners * slots

    @pl.when(pl.program_id(0) == 0)
    def _():
        field = lax.broadcasted_iota(jnp.int32, (fields, fields), 0)
        place[...] = jnp.where(field == slot_row[...], 1.0, 0.0).astype(BF)

    x = nn(place[...], rec[:, 0].reshape(fields, width)).astype(BF)
    embeds[0] = x
    c = tn(x, proj_y[...]).astype(BF)
    crossed[0] = c
    m = nn(proj_p[...], x).astype(BF)
    mixing[0] = m
    v = nn(m, c)
    inter[...] = v
    unit, _ = layer_norm(v)
    rows[...] = (unit * gain[...]).astype(BF)


def front(received, slot_field, proj_y, proj_p, gain, filled, samples, start, deps, name):
    owners, here, slots, width = received.shape
    fields, rank = proj_y.shape
    made = proj_p.shape[0]
    return pl.pallas_call(
        ordered(front_kernel, 5 + len(filled), deps),
        grid=(here,),
        in_specs=[
            pl.BlockSpec((owners, 1, slots, width), lambda b: (0, b, 0, 0)),
            const(1, fields),
            const(fields, rank),
            const(made, fields),
            const(1, rank),
        ]
        + unread(filled)
        + unread(deps),
        out_specs=[
            by_sample(1, fields, width),
            from_sample(start, 1, width, rank),
            from_sample(start, 1, made, width),
            from_sample(start, made, rank),
            by_sample(made, rank),
        ],
        out_shape=[
            jax.ShapeDtypeStruct((here, fields, width), BF),
            pltpu.HBM((samples, width, rank), BF),
            pltpu.HBM((samples, made, width), BF),
            pltpu.HBM((samples * made, rank), F32),
            jax.ShapeDtypeStruct((here * made, rank), BF),
        ],
        input_output_aliases={5: 1, 6: 2, 7: 3} if filled else {},
        scratch_shapes=[pltpu.VMEM((fields, fields), BF)],
        compiler_params=params(),
        name=name,
    )(received, slot_field[None, :], proj_y, proj_p, gain, *filled, *deps)


def linear_kernel(embeds, linear_w, gain, cot, layer_out, partial):
    made = linear_w.shape[0]
    first = embeds.shape[1] - made
    x = embeds[0]
    summed = nn(linear_w[...], x) + x[first:].astype(F32)
    unit, scale = layer_norm(summed)
    layer_out[0, :first] = jnp.zeros_like(layer_out[0, :first])
    layer_out[0, first:] = (unit * gain[...]).astype(BF)
    grad = norm_back(unit, scale, gain[...], cot[0, first:].astype(F32))
    back = tn(linear_w[...], grad.astype(BF))
    partial[0, :first] = back[:first]
    partial[0, first:] = back[first:] + grad


def linear(embeds, linear_w, gain, cot, deps):
    samples, fields, width = embeds.shape
    return pl.pallas_call(
        ordered(linear_kernel, 4, deps),
        grid=(samples,),
        in_specs=[
            by_sample(1, fields, width),
            const(*linear_w.shape),
            const(1, width),
            by_sample(1, fields, width),
        ]
        + unread(deps),
        out_specs=[by_sample(1, fields, width)] * 2,
        out_shape=[pltpu.HBM(cot.shape, BF), pltpu.HBM(cot.shape, F32)],
        compiler_params=params(),
        name="linear",
    )(embeds, linear_w, gain, cot, *deps)


def activate(gate):
    sig = 0.5 * jnp.tanh(0.5 * gate) + 0.5
    h = gate * sig
    return (h.astype(BF), sig + h * (1.0 - sig))


def tiles_of(weight, others, own, most):
    units, width = weight.shape
    tile = min(most, units)
    steps = units // tile
    specs = [
        pl.BlockSpec(
            (tile, width), lambda g, at, n=n: (jnp.clip(g - n * steps, 0, steps - 1), 0)
        )
        for n in range(own + len(others))
    ]
    return steps, specs


def at_tiles(steps, own, near, refs, work):
    step = pl.program_id(0)
    count = len(refs) // 2 - own

    if own:

        @pl.when(step < steps)
        def _():
            work(refs[0], refs[1])

    for n in range(count):
        fetched, traded = refs[2 * own + n], refs[2 * own + count + n]
        here = jnp.logical_and(step >= (n + own) * steps, step < (n + own + 1) * steps)

        @pl.when(jnp.logical_and(here, near[0] == 0))
        def _(up=fetched, down=traded):
            work(up, down)

        @pl.when(jnp.logical_and(here, near[0] != 0))
        def _(up=traded, down=fetched):
            work(up, down)


def accumulate(out, begun, term):
    @pl.when(pl.program_id(0) == 0)
    def _():
        out[...] = term if begun is None else begun[...] + term

    @pl.when(pl.program_id(0) > 0)
    def _():
        out[...] += term


def up_kernel(steps, own, begun, near, rows, *refs):
    def work(up, down):
        hidden, _ = activate(nt(rows[...], up[...]))
        accumulate(refs[-1], refs[0] if begun else None, nn(hidden, down[...]))

    at_tiles(steps, own, near, refs[begun:-1], work)


def back_kernel(steps, own, begun, near, rows, grads, *refs):
    def work(up, down):
        term = None
        gate, grad = nt(rows[...], up[:PART, :]), nt(grads[...], down[:PART, :])
        for at in range(0, up.shape[0], PART):
            now, grad_now, after = gate, grad, at + PART
            if after < up.shape[0]:
                gate = nt(rows[...], up[after : after + PART, :])
                grad = nt(grads[...], down[after : after + PART, :])
            _, slope = activate(now)
            more = nn((grad_now * slope).astype(BF), up[at:after, :])
            term = more if term is None else term + more
        accumulate(refs[-1], refs[0] if begun else None, term)

    at_tiles(steps, own, near, refs[begun:-1], work)


def mlp(kernel, near, blocks, w_up, w_down, fetched, traded, begun, deps, name, own=True, limit=VMEM_BYTES):
    steps, specs = tiles_of(w_up, fetched, own, 1024)
    begun = [] if begun is None else [begun]
    weights = [w_up, w_down] if own else []
    ins = 1 + len(blocks) + len(begun) + len(weights) + 2 * len(fetched)
    return pl.pallas_call(
        ordered(functools.partial(kernel, steps, int(own), len(begun)), ins, deps),
        grid_spec=pltpu.PrefetchScalarGridSpec(
            num_scalar_prefetch=1,
            grid=(steps * len(specs),),
            in_specs=[const(*block.shape) for block in (*blocks, *begun)]
            + specs[:own] * 2
            + specs[own:] * 2
            + unread(deps),
            out_specs=const(*blocks[0].shape),
        ),
        out_shape=jax.ShapeDtypeStruct(blocks[0].shape, F32),
        compiler_params=params(limit),
        name=name,
    )(near, *blocks, *begun, *weights, *fetched, *traded, *deps)


def top_kernel(ff, embeds, gain, cot, _, layer_out, grad, grad_ff):
    summed = ff[...] + embeds[0].astype(F32)
    unit, scale = layer_norm(summed)
    layer_out[0] = (unit * gain[...]).astype(BF)
    g = norm_back(unit, scale, gain[...], cot[0].astype(F32))
    grad[...] = g
    grad_ff[...] = g.astype(BF)


def top(ff, embeds, gain, cot, layer_out):
    samples, _, width = embeds.shape
    made = ff.shape[0] // samples
    return pl.pallas_call(
        top_kernel,
        grid=(samples,),
        in_specs=[
            by_sample(made, width),
            by_sample(1, made, width),
            const(1, width),
            by_sample(1, made, width),
        ]
        + unread([layer_out]),
        out_specs=[by_sample(1, made, width), by_sample(made, width), by_sample(made, width)],
        out_shape=[
            pltpu.HBM(cot.shape, BF),
            jax.ShapeDtypeStruct(ff.shape, F32),
            jax.ShapeDtypeStruct(ff.shape, BF),
        ],
        input_output_aliases={4: 0},
        compiler_params=params(),
        name="top",
    )(ff, embeds, gain, cot, layer_out)


def fill(blocks, out):
    at = 0
    for block in blocks:
        out[at : at + block.shape[0]] = block[...]
        at += block.shape[0]


def weight_kernel(blocks, _, *refs):
    w_up, w_down, grad_down, grad_up, rows, grads = refs[2 * blocks :]

    @pl.when(pl.program_id(0) == 0)
    def _():
        fill(refs[:blocks], rows)
        fill(refs[blocks : 2 * blocks], grads)

    shares, units, width = grad_down.shape
    up = w_up[...].reshape(shares * units, width)
    down = w_down[...].reshape(shares * units, width)
    hidden, slope = activate(nt(up, rows[...]))
    gated = (nt(down, grads[...]) * slope).astype(BF)
    for out, left, right in ((grad_down, hidden, grads), (grad_up, gated, rows)):
        out[...] = nn(left, right[...]).reshape(shares, units, width).astype(out.dtype)


def weight_grads(at, rows, grads, w_up, w_down, kind, deps, name):
    shares, _, units, width = w_up.shape
    blocks = len(rows)
    count = sum(block.shape[0] for block in rows)
    step = max(1, min(shares, 1024 // units if count <= 1024 else 128 // units))
    shared = pl.BlockSpec((step, 1, units, width), lambda g, at: (g, at[0], 0, 0))
    given = pl.BlockSpec((step, units, width), lambda g, at: (g, 0, 0))
    return pl.pallas_call(
        ordered(functools.partial(weight_kernel, blocks), 1 + 2 * blocks + 2, deps),
        grid_spec=pltpu.PrefetchScalarGridSpec(
            num_scalar_prefetch=1,
            grid=(shares // step,),
            in_specs=[const(*block.shape) for block in (*rows, *grads)]
            + [shared, shared]
            + unread(deps),
            out_specs=[given, given],
            scratch_shapes=[pltpu.VMEM((count, width), BF)] * 2,
        ),
        out_shape=[jax.ShapeDtypeStruct((shares, units, width), kind)] * 2,
        compiler_params=params(WIDE_BYTES),
        name=name,
    )(at, *rows, *grads, w_up, w_down, *deps)


def split_kernel(count, each, at, *refs):
    ins, outs = refs[: -count * len(each)], refs[-count * len(each) :]
    for k in reversed(range(count)):
        here = lax.rem(at[0] + k, count)
        first = 0
        for n, terms in enumerate(each):
            total = ins[first][:, here].astype(F32)
            for ref in ins[first + 1 : first + terms]:
                total = total + ref[:, here].astype(F32)
            out = outs[n * count + k]
            out[...] = total.astype(out.dtype)
            first += terms


def split_sum(at, count, sums, kind, deps, name):
    outs = []
    for arrays in sums:
        before, _, units, width = arrays[0].shape
        outs += [((before, units, width), kind if k == 0 else BF) for k in range(count)]
    each = [len(arrays) for arrays in sums]
    pieces = whole(
        ordered(functools.partial(split_kernel, count, each), 1 + sum(each), deps),
        outs,
        name,
        in_specs=[pl.BlockSpec(memory_space=pltpu.SMEM)]
        + [pl.BlockSpec(memory_space=pltpu.VMEM)] * sum(each)
        + unread(deps),
    )(at, *[array for arrays in sums for array in arrays], *deps)
    return [pieces[n * count : (n + 1) * count] for n in range(len(sums))]


def join_kernel(at, *refs):
    ins, out = refs[:-1], refs[-1]
    count = len(ins)
    for k, ref in enumerate(ins):
        out[:, lax.rem(at[0] + (count - k), count)] = ref[...].astype(out.dtype)


def join(at, arrays, kind, deps, name):
    before, units, width = arrays[0].shape
    (out,) = whole(
        ordered(join_kernel, 1 + len(arrays), deps),
        [((before, len(arrays), units, width), kind)],
        name,
        in_specs=[pl.BlockSpec(memory_space=pltpu.SMEM)]
        + [pl.BlockSpec(memory_space=pltpu.VMEM)] * len(arrays)
        + unread(deps),
    )(at, *arrays, *deps)
    return out


def join_last_kernel(count, _, *refs):
    for piece, out in zip(refs[:count], refs[-count:]):
        out[:, 0] = piece[...].astype(F32)


def join_last(at, pieces, filled, name):
    before, units, width = pieces[0].shape
    count = len(pieces)
    step = max(1, before // 2)
    return pl.pallas_call(
        functools.partial(join_last_kernel, count),
        grid_spec=pltpu.PrefetchScalarGridSpec(
            num_scalar_prefetch=1,
            grid=(before // step,),
            in_specs=[pl.BlockSpec((step, units, width), lambda g, at: (g, 0, 0))] * count
            + unread(filled),
            out_specs=[pl.BlockSpec((step, 1, units, width), lambda g, at: (g, at[0], 0, 0))] * count,
        ),
        out_shape=[pltpu.HBM((before, 2, units, width), F32)] * count,
        input_output_aliases={1 + count + n: n for n in range(len(filled))},
        compiler_params=params(),
        name=name,
    )(at, *pieces, *filled)


def tail_kernel(
    upstream, inter, gain, crossed, mixing, grad_top, partial, proj_y, proj_p, slot_col, *refs
):
    out, place = refs[-2:]
    owners, _, slots, width = out.shape
    fields = owners * slots
    made = mixing.shape[1]

    @pl.when(pl.program_id(0) == 0)
    def _():
        field = lax.broadcasted_iota(jnp.int32, (fields, fields), 1)
        place[...] = jnp.where(field == slot_col[...], 1.0, 0.0).astype(BF)

    unit, scale = layer_norm(inter[...])
    grad_inter = norm_back(unit, scale, gain[...], upstream[...]).astype(BF)
    grad_mixing = nt(grad_inter, crossed[0]).astype(BF)
    grad_crossed = tn(mixing[0], grad_inter).astype(BF)
    grad = partial[0] + tn(proj_p[...], grad_mixing) + nt(proj_y[...], grad_crossed)
    head = (grad[:made] + grad_top[...]).astype(BF)
    grad = jnp.concatenate([head, grad[made:].astype(BF)], axis=0)
    out[:, 0] = nn(place[...], grad).astype(BF).reshape(owners, slots, width)


def tail(upstream, kept, gain, proj_y, proj_p, slot_field, owners, deps):
    inter, crossed, mixing, grad_top, partial = kept
    samples, fields, width = partial.shape
    rank = proj_y.shape[1]
    made = mixing.shape[1]
    slots = fields // owners
    return pl.pallas_call(
        ordered(tail_kernel, 10, deps),
        grid=(samples,),
        in_specs=[
            by_sample(made, rank),
            by_sample(made, rank),
            const(1, rank),
            by_sample(1, width, rank),
            by_sample(1, made, width),
            by_sample(made, width),
            by_sample(1, fields, width),
            const(fields, rank),
            const(made, fields),
            const(fields, 1),
        ]
        + unread(deps),
        out_specs=pl.BlockSpec((owners, 1, slots, width), lambda b: (0, b, 0, 0)),
        out_shape=jax.ShapeDtypeStruct((owners, samples, slots, width), BF),
        scratch_shapes=[pltpu.VMEM((fields, fields), BF)],
        compiler_params=params(),
        name="tail",
    )(
        upstream,
        inter,
        gain,
        crossed,
        mixing,
        grad_top,
        partial,
        proj_y,
        proj_p,
        slot_field[:, None],
        *deps,
    )


def whole(kernel, shapes, name, **options):
    return pl.pallas_call(
        kernel,
        out_shape=[jax.ShapeDtypeStruct(shape, kind) for shape, kind in shapes],
        compiler_params=params(),
        name=name,
        **options,
    )


def turn(value, axis, size, shift):
    return lax.ppermute(value, axis, [(i, (i + shift) % size) for i in range(size)])


def after(value, *others):
    return lax.optimization_barrier((value, *others))[0]


def body(
    sizes,
    tables,
    bag_ids,
    bag_lengths,
    slot_field,
    proj_y,
    proj_p,
    linear_w,
    fm_gain,
    w_up,
    w_down,
    out_gain,
    cotangent,
):
    wide = sizes["wide"]
    emb = tuple(axis for axis in sizes if axis != "wide")
    owners = 2 ** len(emb)
    width = tables.shape[2]
    made = proj_p.shape[0]
    cot = cotangent[0]
    samples = cot.shape[0]
    gain_fm, gain_out = fm_gain[None, :], out_gain[None, :]
    places = {axis: lax.axis_index(axis).astype(jnp.int32)[None] for axis in emb}

    *outer, mid, near = emb

    def spread(value):
        return [turn(value, "wide", wide, k) for k in range(1, wide)]

    def exchange(value):
        flat = value.reshape(owners * samples, *value.shape[2:])
        moved = lax.all_to_all(flat, emb, split_axis=0, concat_axis=0, tiled=True)
        return moved.reshape(value.shape)

    fetched = spread(lax.select(places[near][0] == 0, w_up, w_down))
    (pooled,) = pool_bags(tables, bag_ids[0], bag_lengths[0], owners, 1)
    received = exchange(pooled)
    embeds, crossed, mixing, inter, rows = front(
        received, slot_field, proj_y, proj_p, gain_fm, [], samples, 0, [], "front"
    )
    all_rows = [rows, *spread(rows)]
    fetched, _ = lax.optimization_barrier((fetched, rows))
    traded = [turn(weight, near, 2, 1) for weight in fetched]
    layer_out, partial = linear(embeds, linear_w, gain_out, cot, [rows])
    ff = mlp(up_kernel, places[near], [rows], w_up, w_down, [], [], None, [partial], "up_own")
    ff = mlp(up_kernel, places[near], [rows], w_up, w_down, fetched, traded, ff, [], "up_other", False)
    layer_out, grad_top, grads = top(ff, embeds, gain_out, cot, layer_out)
    all_grads = [grads, *spread(grads)]

    units = w_up.shape[0] // owners
    shared = (owners // 2, 2, units, width)
    shares = (w_up.reshape(shared), w_down.reshape(shared))
    upstream = mlp(
        back_kernel,
        places[near],
        [rows, grads],
        w_up,
        w_down,
        fetched,
        traded,
        None,
        [],
        "back",
        limit=WIDE_BYTES,
    )
    slot_grads = tail(
        upstream,
        (inter, crossed, mixing, grad_top, partial),
        gain_fm,
        proj_y,
        proj_p,
        slot_field,
        owners,
        [*all_rows[1:], *all_grads[1:]],
    )
    returned = exchange(slot_grads)
    away = weight_grads(1 - places[near], all_rows, all_grads, *shares, BF, [slot_grads], "weights_1")
    arrived = [turn(part, near, 2, 1) for part in away]
    kept_parts = weight_grads(places[near], all_rows, all_grads, *shares, BF, [away[0]], "weights_0")
    last = [kept_parts[0]]
    sums = [list(terms) for terms in zip(kept_parts, arrived)]

    orders = [(*outer, mid, near), (*outer[:1], mid, *outer[1:], near)]
    left = [list(emb[:-1]), list(emb[:-1])]

    def halve(n, step):
        nonlocal last
        axis = orders[n][step]
        before = 2 ** left[n].index(axis)
        left[n].remove(axis)
        terms = [term.reshape(before, 2, -1, width) for term in sums[n]]
        name = f"{('down', 'up')[n]}_split_{axis}"
        ((keep, away),) = split_sum(places[axis], 2, [terms], F32, last, name)
        last = [away]
        sums[n] = [keep, turn(away, axis, 2, 1)]

    for step in range(len(emb) - 2, -1, -1):
        halve(0, step)
        halve(1, step)
        if step == len(emb) - 2:
            last = [*last, returned]
    weights = []
    for n, name in enumerate(("down", "up")):
        terms = [term.reshape(1, 1, units, width) for term in sums[n]]
        ((share,),) = split_sum(places[near], 1, [terms], BF, last, f"{name}_share")
        last = [share]
        weights.append(share.reshape(-1, width))
    done = [[], []]
    for step in range(len(emb) - 1):
        for n, name in enumerate(("down", "up")):
            axis = orders[n][step]
            at = emb.index(axis)
            before = 2 ** sum(emb.index(other) < at for other in done[n])
            value = weights[n].reshape(before, -1, width)
            other = turn(value, axis, 2, 1)
            joined = join(places[axis], [value, other], BF, last, f"{name}_join_{axis}")
            last = [joined]
            weights[n] = joined.reshape(-1, width)
            done[n].append(axis)
    mine = [value.reshape(owners // 2, units, width) for value in weights]
    others = [turn(value, near, 2, 1) for value in mine]
    joined = join_last(places[near], mine, [], "weights_mine")
    joined = join_last(1 - places[near], others, joined, "weights_others")
    down, up = [value.reshape(-1, width) for value in joined]
    return (layer_out[None], returned.reshape(1, owners * samples, -1, width), up, down)


def solution(mesh):
    emb, wide = mesh.shape["emb"], mesh.shape["wide"]
    names = tuple(f"emb_{k}" for k in range(emb.bit_length() - 1))
    split = Mesh(mesh.devices.reshape((2,) * len(names) + (wide,)), (*names, "wide"))
    return jax.shard_map(
        functools.partial(body, dict(split.shape)),
        mesh=split,
        in_specs=(
            P(names, None, None),
            P("wide", None, names, None),
            P("wide", None, names),
            P(),
            P(),
            P(),
            P(),
            P(),
            P("wide", None),
            P("wide", None),
            P(),
            P("wide", names, None, None),
        ),
        out_specs=(
            P("wide", names, None, None),
            P("wide", None, names, None),
            P("wide", None),
            P("wide", None),
        ),
        check_vma=False,
    )
```
